256 devices in a mesh: node: 64 (over x, z, core), local: 4 (over y).
Axes of the slice: x: 4, y: 4, z: 8, core: 2. Of those that a mesh axis runs over, the one named last changes fastest.
Arguments:
- grad_partials: bfloat16 [64, 460, 14848], P('node', None, 'local'), may hold values from -6 to 6
- old_master: float32 [64, 8, 14848], P('node', None, 'local'), may hold values from -6 to 6
- old_first: float32 [64, 8, 14848], P('node', None, 'local'), may hold values from -16 to 16
- old_second: float32 [64, 8, 14848], P('node', None, 'local'), may hold values from 1 to 100
- old_bounds: int32 [65], replicated, may hold values from 0 to 460, as said below
- new_bounds: int32 [53], replicated, may hold values from 0 to 460, as said below
- step_count: int32 [1], replicated, may hold values from 1 to 20
- learning_rate: float32 [1], replicated, may hold values from 0.05 to 0.4
Outputs:
- new_master: float32 [64, 12, 14848], P('node', None, 'local')
- new_first: float32 [64, 12, 14848], P('node', None, 'local')
- new_second: float32 [64, 12, 14848], P('node', None, 'local')
- secondary: bfloat16 [460, 14848], P('local')
The draws below stay inside these ranges and needn't reach their ends.
Inputs may be any that keep to these rules, and one draw needn't show every extreme that they name: Increasing from 0 to 460, every entry a multiple of 4; each old owner holds 4 or 8 units, and some owner holds 8; slots of old_master, old_first and old_second past an owner's units belong to no unit. Between two successive entries of old_bounds and new_bounds taken together lie exactly 4 units, and no entry but the first and the last is in both, so one old owner hands at most 4 units to one new owner, and some pair hands exactly 4. `new_bounds`: increasing from 0 to 460, every entry a multiple of 4; each new owner holds 8 to 12 units, and some owner holds 12.
All inputs are finite; a program needn't handle non-finite values.
Results may differ from the reference program's by a relative error of at most 0.001.
Values may be sent and summed in bfloat16 or wider, within the bound.
A program may use at most 128 MiB of HBM per device.

```python
import math
import jax
import jax.numpy as jnp
from jax import lax

SEG = 4
UNIT = 14848
NEW_NODES = 52
UNITS = 460
CAP_OLD = 8
CAP_NEW = 12
N_NODE = 64


def merged_layout(key):
    segments = UNITS // SEG
    order = jax.random.permutation(key, NEW_NODES)
    inside = 1 + (order < N_NODE - 1 - NEW_NODES).astype(jnp.int32)
    new_points = jnp.concatenate([jnp.zeros((1,), jnp.int32), jnp.cumsum(inside + 1).astype(jnp.int32)])
    marks = jnp.arange(segments + 1).astype(jnp.int32)
    is_new = jnp.any(marks[:, None] == new_points[None, 1:NEW_NODES], axis=1).astype(jnp.int32)
    scores = is_new * (2 * (segments + 1)) + marks
    old_points = jnp.argsort(scores, stable=True)[:N_NODE + 1].astype(jnp.int32)
    return (old_points * SEG, new_points * SEG)


def draw_old_bounds(key, part):
    shared = merged_layout(key)
    return shared[0].astype(jnp.int32)


def draw_new_bounds(key, part):
    shared = merged_layout(key)
    return shared[1].astype(jnp.int32)


def strengthened(result, rng, source, target, parts, factor):
    owner, partner = [(jnp.arange(result.shape[position]) // (result.shape[position] // parts)).reshape([-1 if axis == position else 1 for axis in range(result.ndim)]) for position in (source, target)]
    chosen = jax.random.permutation(rng, parts)[partner]
    strong = (owner == chosen) | (owner == (partner + parts // 2) % parts)
    return jnp.where(strong, factor * result, result)


def levels(key, shape, split, smallest, largest):
    def one(dim, shards_of):
        draws = jax.random.uniform(jax.random.fold_in(jax.random.fold_in(key, 6), dim), (shards_of,), jnp.float32, smallest / len(split), largest / len(split))
        return jnp.repeat(jnp.exp(draws), shape[dim] // shards_of).reshape((-1,) + (1,) * (len(shape) - dim - 1))

    loudness = one(*split[0])
    for cut in split[1:]:
        loudness = loudness * one(*cut)
    return loudness


def noise(key, shape, deviation, limit, split=(), held_as=jnp.bfloat16):
    gain = levels(key, shape, split, -0.22, 0.18) if split else 1.0
    drawn = jax.random.normal(key, shape, jnp.float32) * deviation * gain
    return jnp.minimum(jnp.maximum(drawn, -limit), limit).astype(held_as)


def bell_draw_with(rng, extent, deviation, most, cuts, heavy, held_as=jnp.bfloat16):
    array = deviation * jax.random.normal(rng, extent, jnp.float32)
    if cuts:
        array = array * levels(rng, extent, cuts, -0.22, 0.18)
    return jnp.clip(strengthened(array, jax.random.fold_in(rng, 3), *heavy), -most, most).astype(held_as)


def setup_inputs(seed: int = 0) -> dict:
    key_of = jax.random.split(jax.random.key(seed), 9)
    grad_partials = bell_draw_with(key_of[0], (N_NODE, UNITS, UNIT), 1.0, 6.0, ((0, 64), (2, 4)), (0, 1, 4, 2.0))
    old_master = noise(key_of[1], (N_NODE, CAP_OLD, UNIT), 1.0, 6.0, ((0, 64), (2, 4)), jnp.float32)
    old_first = noise(key_of[2], (N_NODE, CAP_OLD, UNIT), 3.0, 16.0, ((0, 64), (2, 4)), jnp.float32)
    old_second = jnp.clip(jnp.exp(math.log(100.0) - 4.6051702 * jax.random.uniform(key_of[3], (N_NODE, CAP_OLD, UNIT), jnp.float32) ** levels(key_of[3], (N_NODE, CAP_OLD, UNIT), ((0, 64), (2, 4)), -0.2, 0.2)), 1.0, 100.0)
    old_bounds = draw_old_bounds(jax.random.fold_in(key_of[8], 71), 0)
    new_bounds = draw_new_bounds(jax.random.fold_in(key_of[8], 71), 0)
    step_count = jax.random.randint(key_of[6], (1,), 1, 21).astype(jnp.int32)
    learning_rate = jnp.clip(jnp.exp(jax.random.uniform(key_of[7], (1,), jnp.float32, math.log(0.05), math.log(0.4))), 0.05, 0.4)
    return {"grad_partials": grad_partials, "old_master": old_master, "old_first": old_first, "old_second": old_second, "old_bounds": old_bounds, "new_bounds": new_bounds, "step_count": step_count, "learning_rate": learning_rate}


beta_first = 0.9
beta_second = 0.95
adam_eps = 1e-08
decay = 0.1

def owner_index(bounds, unit_ids):
    owners = bounds.shape[0] - 1
    return lax.optimization_barrier(jnp.sum((bounds[None, 1:owners] <= unit_ids[:, None]).astype(jnp.int32), axis=1)).astype(jnp.int32)

def adam_update(master, first, second, gradient, step_count, learning_rate):
    steps_taken = step_count[0].astype(jnp.float32)
    first_new = beta_first * first + (1.0 - beta_first) * gradient
    second_new = beta_second * second + (1.0 - beta_second) * gradient * gradient
    first_hat = first_new / (1.0 - jnp.power(jnp.float32(beta_first), steps_taken))
    second_hat = second_new / (1.0 - jnp.power(jnp.float32(beta_second), steps_taken))
    master_new = master - learning_rate[0] * (first_hat / (jnp.sqrt(second_hat) + adam_eps) + decay * master)
    return (master_new, first_new, second_new)

def reference(grad_partials, old_master, old_first, old_second, old_bounds, new_bounds, step_count, learning_rate):
    unit_ids = jnp.arange(UNITS).astype(jnp.int32)
    owners = owner_index(old_bounds, unit_ids)
    slot_of = (unit_ids - old_bounds[owners]).astype(jnp.int32)
    master = old_master[owners, slot_of]
    first = old_first[owners, slot_of]
    second = old_second[owners, slot_of]
    gradient = lax.optimization_barrier(jnp.sum(grad_partials.astype(jnp.float32), axis=0))
    updated = adam_update(master, first, second, gradient, step_count, learning_rate)
    node_ids = jnp.arange(N_NODE).astype(jnp.int32)[:, None]
    owner_ids = ((N_NODE // 2 - node_ids) % N_NODE).astype(jnp.int32)
    slot_ids = jnp.arange(CAP_NEW).astype(jnp.int32)[None, :]
    begin = new_bounds[jnp.minimum(owner_ids, NEW_NODES)]
    finish = new_bounds[jnp.minimum(owner_ids + 1, NEW_NODES)]
    wanted = begin + slot_ids
    usable = (owner_ids < NEW_NODES) & (wanted < finish)
    clipped = jnp.clip(wanted, 0, UNITS - 1).astype(jnp.int32)
    placed = tuple((jnp.where(usable[:, :, None], member[clipped], 0.0) for member in updated))
    secondary = updated[0].astype(jnp.bfloat16)
    return (placed[0], placed[1], placed[2], secondary)
```

```python
import jax
import jax.numpy as jnp
from jax import lax
from jax.experimental import pallas as pl
from jax.experimental.pallas import tpu as pltpu
from jax.sharding import PartitionSpec as P

MESH = pl.DeviceIdType.MESH
F32, BF16, I16, I32 = jnp.float32, jnp.bfloat16, jnp.int16, jnp.int32

UNITS = 460
WIDTH = 3712
LANE = 128
TILES = WIDTH // LANE
NODES = 64
CHIPS = 32
NX, NZ, NY = 4, 8, 4
HALF = 240
SECOND = 224
CHUNKS, ROWS = 3, 80
SEGMENTS = 115
CAP_NEW = 12
OWNERS = 52
PART = 64
LEVEL = 32760.0

beta_first = 0.9
beta_second = 0.95
adam_eps = 1e-08
decay = 0.1


def power(base, steps):
    result = jnp.float32(1.0)
    factor = float(base)
    for bit in range(5):
        result = jnp.where((steps // (1 << bit)) % 2 == 1, result * jnp.float32(factor), result)
        factor = factor * factor
    return result


def encode(value, inverse):
    return jnp.round(value * inverse).astype(I32).astype(I16)


def decode(code, scale):
    return code.astype(I32).astype(F32) * scale


def kernel(
    ob, nb, step_count, learning_rate, g, om, of, os_,
    o_m, o_f, o_s, o_w,
    gb, raw, summed, xsnd, xscl, xr, xs, zsum, zsnd, zscl, zr, zs, both,
    stg, st, mat, new, wb, blocks, snd, r2,
    raw_s, raw_r, xd_s, xd_r, xc_s, xc_r, zd_s, zd_r, zc_s, zc_r, gc_s, gc_r,
    s1_s, s1_r, st_s, st_r, w1_s, w1_r, w2_s, w2_r, rt_s, rt_r, lf_s, lf_r,
    rr_s, rr_r, rl_s, rl_r, cx_s, cx_r, s2_s, s2_r,
):
    node, y = lax.axis_index("node"), lax.axis_index("local")
    c, chip = node % 2, node // 2
    x, z = chip // NZ, chip % NZ

    def send(src, dst, ss, rs, to_chip, to_core=None, to_y=None):
        core = c if to_core is None else to_core
        return pltpu.make_async_remote_copy(
            src_ref=src, dst_ref=dst, send_sem=ss, recv_sem=rs,
            device_id=(to_chip * 2 + core, y if to_y is None else to_y), device_id_type=MESH,
        )

    sent = []

    def start(copy):
        copy.start()
        sent.append(copy)
        return copy

    barrier = pltpu.get_barrier_semaphore()

    def greet(d, carry):
        pl.semaphore_signal(barrier, inc=1, device_id=(((chip + d) % CHIPS) * 2 + c, y), device_id_type=MESH)
        return carry

    lax.fori_loop(1, CHIPS, greet, 0)
    pl.semaphore_signal(barrier, inc=1, device_id=(chip * 2 + 1 - c, y), device_id_type=MESH)
    for d in range(1, NY):
        pl.semaphore_signal(barrier, inc=1, device_id=(node, (y + d) % NY), device_id_type=MESH)

    def stage(t, carry):
        col = pl.ds(pl.multiple_of(t * LANE, LANE), LANE)
        gb[t, 0:448] = g[0, 0:448, col]
        gb[t, 448:464] = jnp.zeros((16, LANE), BF16)
        gb[t, 448:460] = g[0, 448:460, col]
        stg[t, 0] = om[0, :, col]
        stg[t, 1] = of[0, :, col]
        stg[t, 2] = os_[0, :, col]
        return carry

    lax.fori_loop(0, TILES, stage, 0)
    for t in range(TILES, CHIPS):
        stg[t] = jnp.zeros((3, 8, LANE), F32)
        xsnd[3, :, t - 24] = jnp.zeros((CHUNKS, ROWS, LANE), I16)

    pl.semaphore_wait(barrier, CHIPS - 1 + 1 + NY - 1)

    base, other = c * SECOND, (1 - c) * SECOND
    raws = []
    for k in range(CHUNKS):
        rows = pl.ds(pl.multiple_of(other + ROWS * k, 16), ROWS)
        raws.append(start(send(gb.at[:, rows], raw.at[k], raw_s.at[k], raw_r.at[k], chip, 1 - c)))

    def state_out(d, carry):
        to = (chip + d) % CHIPS
        send(stg.at[to], st.at[c, chip], s1_s, s1_r, to).start()
        return carry

    lax.fori_loop(1, CHIPS, state_out, 0)
    pltpu.make_async_copy(stg.at[chip], st.at[c, chip], s1_r).start()

    xcopies = []
    for k in range(CHUNKS):
        raws[k].wait_recv()
        rows = pl.ds(pl.multiple_of(base + ROWS * k, 16), ROWS)

        def add(t, top):
            value = gb[t, rows].astype(F32) + raw[k, t].astype(F32)
            summed[t] = value
            return jnp.maximum(top, jnp.abs(value))

        top = lax.fori_loop(0, TILES, add, jnp.zeros((ROWS, LANE), F32))
        top = jnp.maximum(jnp.max(top, axis=0, keepdims=True), 1e-30)
        xscl[k] = top / LEVEL
        inverse = LEVEL / top

        def code(t, carry):
            xsnd[t // NZ, k, t % NZ] = encode(summed[t], inverse)
            return carry

        lax.fori_loop(0, TILES, code, 0)
        for d in range(1, NX):
            gx = (x + d) % NX
            to = gx * NZ + z
            xcopies.append((
                start(send(xsnd.at[gx, k], xr.at[d - 1, k], xd_s.at[d - 1, k], xd_r.at[d - 1, k], to)),
                start(send(xscl.at[k], xs.at[d - 1, k], xc_s.at[d - 1, k], xc_r.at[d - 1, k], to)),
            ))

    zcopies = []
    for k in range(CHUNKS):
        for pair in xcopies[3 * k : 3 * k + 3]:
            pair[0].wait_recv()
            pair[1].wait_recv()

        def add_x(t, top):
            value = decode(xsnd[x, k, t], xscl[k])
            for d in range(NX - 1):
                value = value + decode(xr[d, k, t], xs[d, k])
            zsum[k, t] = value
            return jnp.maximum(top, jnp.abs(value))

        top = lax.fori_loop(0, NZ, add_x, jnp.zeros((ROWS, LANE), F32))
        top = jnp.maximum(jnp.max(top, axis=0, keepdims=True), 1e-30)
        zscl[k] = top / LEVEL
        inverse = LEVEL / top

        def code_z(t, carry):
            zsnd[k, t] = encode(zsum[k, t], inverse)
            return carry

        lax.fori_loop(0, NZ, code_z, 0)
        for d in range(1, NZ):
            gz = (z + d) % NZ
            to = x * NZ + gz
            zcopies.append((
                start(send(zsnd.at[k, gz], zr.at[d - 1, k], zd_s.at[d - 1, k], zd_r.at[d - 1, k], to)),
                start(send(zscl.at[k], zs.at[d - 1, k], zc_s.at[d - 1, k], zc_r.at[d - 1, k], to)),
            ))

    pltpu.make_async_copy(st.at[c], st.at[c], s1_r).wait()
    st_copy = start(send(st.at[c], st.at[c], st_s, st_r, chip, 1 - c))

    gcopies = []
    for k in range(CHUNKS):
        for pair in zcopies[7 * k : 7 * k + 7]:
            pair[0].wait_recv()
            pair[1].wait_recv()
        value = zsum[k, z]
        for d in range(NZ - 1):
            value = value + decode(zr[d, k], zs[d, k])
        rows = pl.ds(ROWS * k, ROWS)
        both[c, rows] = value
        gcopies.append(start(send(both.at[c, rows], both.at[c, rows], gc_s.at[k], gc_r.at[k], chip, 1 - c)))

    st_copy.wait_recv()
    for a in range(3):
        mat[a, 456:480] = jnp.zeros((24, LANE), F32)
        new[a, 464:480] = jnp.zeros((16, LANE), F32)

    def place(s, i):
        i = jnp.minimum(i + (ob[i + 1] <= 4 * s).astype(I32), NODES - 1)
        offset = jnp.clip(4 * s - ob[i], 0, 4)
        for a in range(3):
            mat[a, pl.ds(4 * s, 4)] = st[i % 2, i // 2, a, pl.ds(offset, 4)]
        return i

    lax.fori_loop(0, SEGMENTS, place, jnp.int32(0))

    for copy in gcopies:
        copy.wait_recv()

    steps = step_count[0]
    rate = learning_rate[0]
    first_left = 1.0 - power(beta_first, steps)
    second_left = 1.0 - power(beta_second, steps)

    def step(half, shift):
        def body(b, carry):
            rows = pl.ds(pl.multiple_of(b * 8, 8), 8)
            gradient = both[half, pl.ds(pl.multiple_of(b * 8 - shift, 8), 8)]
            master = mat[0, rows]
            first_new = beta_first * mat[1, rows] + (1.0 - beta_first) * gradient
            second_new = beta_second * mat[2, rows] + (1.0 - beta_second) * gradient * gradient
            first_hat = first_new / first_left
            second_hat = second_new / second_left
            new[0, rows] = master - rate * (first_hat / (jnp.sqrt(second_hat) + adam_eps) + decay * master)
            new[1, rows] = first_new
            new[2, rows] = second_new
            return carry

        return body

    lax.fori_loop(0, 29, step(0, 0), 0)
    lax.fori_loop(29, 58, step(1, SECOND), 0)

    for q in range(NY):
        wb[q] = new[0, 115 * q : 115 * q + 128].astype(BF16)
    mine = pl.ds(pl.multiple_of(c * PART, PART), PART)
    w1 = []
    for d in range(1, NY):
        to = (y + d) % NY
        w1.append(start(send(wb.at[to, mine], blocks.at[c, chip, y], w1_s.at[d - 1], w1_r.at[d - 1], chip, to_y=to)))
    blocks[c, chip, y] = wb[y, mine]

    def pick(m, carry):
        begin = jnp.clip(nb[2 * m + c], 0, UNITS)
        count = nb[2 * m + c + 1] - begin
        slot = lax.broadcasted_iota(I32, (CAP_NEW, LANE), 0)
        for a in range(3):
            rows = new[a, pl.ds(begin, CAP_NEW)]
            snd[m, CAP_NEW * a : CAP_NEW * (a + 1)] = jnp.where(slot < count, rows, 0.0)
        return carry

    lax.fori_loop(0, OWNERS // 2, pick, 0)

    for copy in w1:
        copy.wait_recv()
    w2 = []
    for d in range(1, NZ):
        to = x * NZ + (z + d) % NZ
        w2.append(start(send(blocks.at[c, chip], blocks.at[c, chip], w2_s.at[d - 1], w2_r.at[d - 1], to)))
    right, left = ((x + 1) % NX) * NZ, ((x + 3) % NX) * NZ
    across = ((x + 2) % NX) * NZ
    from_left, from_right = [], []

    def share(slot, e):
        start(send(blocks.at[c, slot], blocks.at[c, slot], cx_s.at[e], cx_r, chip, 1 - c))

    def spread(e):
        slot = x * NZ + (z + NZ - e) % NZ
        from_left.append(start(send(blocks.at[c, slot], blocks.at[c, slot], rt_s.at[e], rt_r.at[e], right + z)))
        from_right.append(start(send(blocks.at[c, slot], blocks.at[c, slot], lf_s.at[e], lf_r.at[e], left + z)))
        share(slot, e)

    spread(0)

    owner = (48 - c - chip) % CHIPS

    def owners_out(d, carry):
        to = (chip + d) % CHIPS
        m = (48 - c - to) % CHIPS

        @pl.when(m < OWNERS // 2)
        def _():
            send(snd.at[m], r2.at[chip], s2_s, s2_r, to).start()

        return carry

    lax.fori_loop(1, CHIPS, owners_out, 0)

    @pl.when(owner < OWNERS // 2)
    def _():
        pltpu.make_async_copy(snd.at[owner], r2.at[chip], s2_r).start()

    relay_left, relay_right = [], []

    def relay(e):
        at = (z + NZ - e) % NZ
        from_left[e].wait_recv()
        half = blocks.at[c, left + at, 0:2]
        relay_left.append(start(send(half, half, rr_s.at[e], rr_r.at[e], right + z)))
        share(left + at, 8 + e)
        from_right[e].wait_recv()
        half = blocks.at[c, right + at, 2:4]
        relay_right.append(start(send(half, half, rl_s.at[e], rl_r.at[e], left + z)))
        share(right + at, 16 + e)

    for e in range(1, NZ):
        w2[e - 1].wait_recv()
        spread(e)
        relay(e - 1)
    relay(NZ - 1)
    for e in range(NZ):
        relay_left[e].wait_recv()
        relay_right[e].wait_recv()
        share(across + (z + NZ - e) % NZ, 24 + e)

    @pl.when(owner < OWNERS // 2)
    def _():
        pltpu.make_async_copy(r2, r2, s2_r).wait()

        def fill(t, carry):
            col = pl.ds(pl.multiple_of(t * LANE, LANE), LANE)
            o_m[0, :, col] = r2[t, 0:12]
            o_f[0, :, col] = r2[t, 12:24]
            o_s[0, :, col] = r2[t, 24:36]
            return carry

        lax.fori_loop(0, TILES, fill, 0)
        pltpu.make_async_copy(snd.at[0:25], snd.at[0:25], s2_s).wait()

    @pl.when(owner >= OWNERS // 2)
    def _():
        for out in (o_m, o_f, o_s):
            out[...] = jnp.zeros_like(out)
        pltpu.make_async_copy(snd.at[0:26], snd.at[0:26], s2_s).wait()

    pltpu.make_async_copy(blocks.at[1 - c], blocks.at[1 - c], cx_r).wait()

    def finish(t, carry):
        for q in range(NY):
            col = pl.ds(pl.multiple_of(q * WIDTH + t * LANE, LANE), LANE)
            o_w[0:64, col] = blocks[0, t, q]
            o_w[64:115, col] = blocks[1, t, q, 0:51]
        return carry

    lax.fori_loop(0, TILES, finish, 0)

    pltpu.make_async_copy(stg.at[0:31], stg.at[0:31], s1_s).wait()
    for copy in sent:
        copy.wait_send()


def on_device(grad_partials, old_master, old_first, old_second, old_bounds, new_bounds, step_count, learning_rate):
    vmem, smem = pl.BlockSpec(memory_space=pltpu.VMEM), pl.BlockSpec(memory_space=pltpu.SMEM)
    dma = pltpu.SemaphoreType.DMA
    state = jax.ShapeDtypeStruct((1, CAP_NEW, WIDTH), F32)
    scratch = [
        pltpu.VMEM((TILES, 464, LANE), BF16),
        pltpu.VMEM((CHUNKS, TILES, ROWS, LANE), BF16),
        pltpu.VMEM((TILES, ROWS, LANE), F32),
        pltpu.VMEM((NX, CHUNKS, NZ, ROWS, LANE), I16),
        pltpu.VMEM((CHUNKS, 1, LANE), F32),
        pltpu.VMEM((NX - 1, CHUNKS, NZ, ROWS, LANE), I16),
        pltpu.VMEM((NX - 1, CHUNKS, 1, LANE), F32),
        pltpu.VMEM((CHUNKS, NZ, ROWS, LANE), F32),
        pltpu.VMEM((CHUNKS, NZ, ROWS, LANE), I16),
        pltpu.VMEM((CHUNKS, 1, LANE), F32),
        pltpu.VMEM((NZ - 1, CHUNKS, ROWS, LANE), I16),
        pltpu.VMEM((NZ - 1, CHUNKS, 1, LANE), F32),
        pltpu.VMEM((2, HALF, LANE), F32),
        pltpu.VMEM((CHIPS, 3, 8, LANE), F32),
        pltpu.VMEM((2, CHIPS, 3, 8, LANE), F32),
        pltpu.VMEM((3, 480, LANE), F32),
        pltpu.VMEM((3, 480, LANE), F32),
        pltpu.VMEM((NY, 128, LANE), BF16),
        pltpu.VMEM((2, CHIPS, NY, PART, LANE), BF16),
        pltpu.VMEM((OWNERS // 2, 40, LANE), F32),
        pltpu.VMEM((CHIPS, 40, LANE), F32),
        dma((CHUNKS,)), dma((CHUNKS,)),
        dma((NX - 1, CHUNKS)), dma((NX - 1, CHUNKS)),
        dma((NX - 1, CHUNKS)), dma((NX - 1, CHUNKS)),
        dma((NZ - 1, CHUNKS)), dma((NZ - 1, CHUNKS)),
        dma((NZ - 1, CHUNKS)), dma((NZ - 1, CHUNKS)),
        dma((CHUNKS,)), dma((CHUNKS,)),
        dma, dma,
        dma, dma,
        dma((NY - 1,)), dma((NY - 1,)),
        dma((NZ - 1,)), dma((NZ - 1,)),
        dma((NZ,)), dma((NZ,)),
        dma((NZ,)), dma((NZ,)),
        dma((NZ,)), dma((NZ,)),
        dma((NZ,)), dma((NZ,)),
        dma((CHIPS,)), dma,
        dma, dma,
    ]
    return pl.pallas_call(
        kernel,
        name="adamw_move",
        out_shape=(state, state, state, jax.ShapeDtypeStruct((115, 4 * WIDTH), BF16)),
        in_specs=[smem, smem, smem, smem, vmem, vmem, vmem, vmem],
        out_specs=(vmem, vmem, vmem, vmem),
        scratch_shapes=scratch,
        compiler_params=pltpu.CompilerParams(collective_id=0, has_side_effects=True, vmem_limit_bytes=56 * 2**20),
    )(old_bounds, new_bounds, step_count, learning_rate, grad_partials, old_master, old_first, old_second)


def solution(mesh):
    split = P("node", None, "local")
    return jax.shard_map(
        on_device,
        mesh=mesh,
        in_specs=(split, split, split, split, P(), P(), P(), P()),
        out_specs=(split, split, split, P("local", None)),
        check_vma=False,
    )
```

```python
import jax
import jax.numpy as jnp
from jax import lax
from jax.experimental import pallas as pl
from jax.experimental.pallas import tpu as pltpu
from jax.sharding import PartitionSpec as P

MESH = pl.DeviceIdType.MESH
F32, BF16, I16, I32 = jnp.float32, jnp.bfloat16, jnp.int16, jnp.int32

UNITS = 460
WIDTH = 3712
LANE = 128
TILES = WIDTH // LANE
NODES = 64
CHIPS = 32
NX, NZ, NY = 4, 8, 4
HALF = 240
SECOND = 224
CHUNKS = ((0, 96), (96, 96), (192, 48))
NC = len(CHUNKS)
SEGMENTS = 115
CAP_NEW = 12
OWNERS = 52
PART = 64
LEVEL = 32760.0

beta_first = 0.9
beta_second = 0.95
adam_eps = 1e-08
decay = 0.1


def power(base, steps):
    result = jnp.float32(1.0)
    factor = float(base)
    for bit in range(5):
        result = jnp.where((steps // (1 << bit)) % 2 == 1, result * jnp.float32(factor), result)
        factor = factor * factor
    return result


def encode(value, inverse):
    return jnp.round(value * inverse).astype(I32).astype(I16)


def decode(code, scale):
    return code.astype(I32).astype(F32) * scale


def kernel(
    ob, nb, step_count, learning_rate, g, end, om, of, os_,
    blocks, r2,
    mine_g, raw, tail, olds, total, acode, right_code, left_code, scl, rscl, lscl,
    a_left, a_right, sa_left, sa_right, f_left, f_right, sf_left, sf_right,
    zsum, zsnd, zscl, zr, zs, both,
    stg, st, mat, new, wb, own, snd, zero,
    in_s, own_g, raw_s, raw_r, a_s, a_r, as_s, as_r, f_s, f_r, fs_s, fs_r, zd_s, zd_r, zc_s, zc_r, gc_s, gc_r,
    s1_s, s1_r, st_s, st_r, w1_s, w1_r, zu_s, zu_r, zd2_s, zd2_r, rt_s, rt_r, lf_s, lf_r,
    rr_s, rr_r, rl_s, rl_r, cx_s, cx_r, s2_s, s2_r, own_s,
):
    node, y = lax.axis_index("node"), lax.axis_index("local")
    c, chip = node % 2, node // 2
    x, z = chip // NZ, chip % NZ

    def send(src, dst, ss, rs, to_chip, to_core=None, to_y=None):
        core = c if to_core is None else to_core
        return pltpu.make_async_remote_copy(
            src_ref=src, dst_ref=dst, send_sem=ss, recv_sem=rs,
            device_id=(to_chip * 2 + core, y if to_y is None else to_y), device_id_type=MESH,
        )

    sent = []

    def start(copy):
        copy.start()
        sent.append(copy)
        return copy

    barrier = pltpu.get_barrier_semaphore()

    def greet(d, carry):
        pl.semaphore_signal(barrier, inc=1, device_id=(((chip + d) % CHIPS) * 2 + c, y), device_id_type=MESH)
        return carry

    lax.fori_loop(1, CHIPS, greet, 0)
    pl.semaphore_signal(barrier, inc=1, device_id=(chip * 2 + 1 - c, y), device_id_type=MESH)
    for d in range(1, NY):
        pl.semaphore_signal(barrier, inc=1, device_id=(node, (y + d) % NY), device_id_type=MESH)

    state_in = [pltpu.make_async_copy(old.at[0], olds.at[a], in_s.at[a]) for a, old in enumerate((om, of, os_))]
    for copy in state_in:
        copy.start()
    row = lax.broadcasted_iota(I32, (16, WIDTH), 0)
    tail[...] = jnp.where(row < 12, end[0].astype(F32), 0.0).astype(BF16)

    @pl.when(c == 0)
    def _():
        pltpu.make_async_copy(g.at[0, 0:HALF], mine_g, own_g).start()

    @pl.when(c == 1)
    def _():
        pltpu.make_async_copy(g.at[0, SECOND:448], mine_g.at[0:224], own_g).start()
        mine_g[224:240] = tail[...]

    for copy in state_in:
        copy.wait()

    def stage(t, carry):
        col = pl.ds(pl.multiple_of(t * LANE, LANE), LANE)
        for a in range(3):
            stg[t, a] = olds[a, :, col]
        return carry

    lax.fori_loop(0, TILES, stage, 0)
    for t in range(TILES, CHIPS):
        total[t] = jnp.zeros((HALF, LANE), F32)

    pl.semaphore_wait(barrier, CHIPS - 1 + 1 + NY - 1)

    @pl.when(c == 0)
    def _():
        for k, (first, rows) in enumerate(CHUNKS):
            rows = min(rows, 224 - first)
            send(g.at[0, SECOND + first : SECOND + first + rows], raw.at[first : first + rows], raw_s.at[k], raw_r.at[k], chip, 1).start()
        send(tail, raw.at[224:240], raw_s.at[NC - 1], raw_r.at[NC - 1], chip, 1).start()

    @pl.when(c == 1)
    def _():
        for k, (first, rows) in enumerate(CHUNKS):
            send(g.at[0, first : first + rows], raw.at[first : first + rows], raw_s.at[k], raw_r.at[k], chip, 0).start()

    @pl.when(c == 0)
    def _():
        pltpu.make_async_copy(mine_g, mine_g, own_g).wait()

    @pl.when(c == 1)
    def _():
        pltpu.make_async_copy(mine_g.at[0:224], mine_g.at[0:224], own_g).wait()

    def state_out(d, carry):
        to = (chip + d) % CHIPS

        @pl.when(to < TILES)
        def _():
            send(stg.at[to], st.at[c, chip], s1_s, s1_r, to).start()

        return carry

    lax.fori_loop(1, CHIPS, state_out, 0)

    @pl.when(chip < TILES)
    def _():
        pltpu.make_async_copy(stg.at[chip], st.at[c, chip], s1_r).start()

    right_x, left_x, far_x = (x + 1) % NX, (x + 3) % NX, (x + 2) % NX
    right_chip, left_chip = right_x * NZ + z, left_x * NZ + z
    acopies, fcopies, zcopies = [], [], []

    def pair(k):
        first, rows = CHUNKS[k]
        at = slice(first, first + rows)
        pltpu.make_async_copy(raw.at[at], raw.at[at], raw_r.at[k]).wait()

        def add(t, top):
            col = pl.ds(pl.multiple_of(t * LANE, LANE), LANE)
            value = mine_g[at, col].astype(F32) + raw[at, col].astype(F32)
            total[t, at] = value
            return jnp.maximum(top, jnp.abs(value))

        top = lax.fori_loop(0, TILES, add, jnp.zeros((rows, LANE), F32))
        top = jnp.maximum(jnp.max(top, axis=0, keepdims=True), 1e-30)
        scl[k] = top / LEVEL
        inverse = LEVEL / top

        def code(t, carry):
            acode[t, at] = encode(total[far_x * NZ + t, at], inverse)
            return carry

        lax.fori_loop(0, NZ, code, 0)
        acopies.append((
            start(send(acode.at[0:4, at], a_left.at[:, at], a_s.at[0, k], a_r.at[0, k], right_chip)),
            start(send(acode.at[4:8, at], a_right.at[:, at], a_s.at[1, k], a_r.at[1, k], left_chip)),
            start(send(scl.at[k], sa_left.at[k], as_s.at[0, k], as_r.at[0, k], right_chip)),
            start(send(scl.at[k], sa_right.at[k], as_s.at[1, k], as_r.at[1, k], left_chip)),
        ))

    def neighbours(k):
        first, rows = CHUNKS[k]
        at = slice(first, first + rows)
        for copy in acopies[k]:
            copy.wait_recv()
        rscl[k] = scl[k] + sa_left[k]
        lscl[k] = scl[k] + sa_right[k]
        to_right, to_left = 1.0 / rscl[k], 1.0 / lscl[k]

        def code(t, carry):
            through = decode(a_left[t, at], sa_left[k])
            right_code[t, at] = encode(total[right_x * NZ + t, at] + through, to_right)
            right_code[t + 4, at] = encode(total[right_x * NZ + t + 4, at], to_right)
            through = decode(a_right[t, at], sa_right[k])
            left_code[t, at] = encode(total[left_x * NZ + t, at], to_left)
            left_code[t + 4, at] = encode(total[left_x * NZ + t + 4, at] + through, to_left)
            return carry

        lax.fori_loop(0, 4, code, 0)
        fcopies.append((
            start(send(right_code.at[:, at], f_left.at[:, at], f_s.at[0, k], f_r.at[0, k], right_chip)),
            start(send(left_code.at[:, at], f_right.at[:, at], f_s.at[1, k], f_r.at[1, k], left_chip)),
            start(send(rscl.at[k], sf_left.at[k], fs_s.at[0, k], fs_r.at[0, k], right_chip)),
            start(send(lscl.at[k], sf_right.at[k], fs_s.at[1, k], fs_r.at[1, k], left_chip)),
        ))

    def along_z(k):
        first, rows = CHUNKS[k]
        at = slice(first, first + rows)
        for copy in fcopies[k]:
            copy.wait_recv()
        zscl[k] = scl[k] + sf_left[k] + sf_right[k]
        inverse = 1.0 / zscl[k]

        def code(t, carry):
            value = total[x * NZ + t, at] + decode(f_left[t, at], sf_left[k]) + decode(f_right[t, at], sf_right[k])
            zsum[t, at] = value
            zsnd[t, at] = encode(value, inverse)
            return carry

        lax.fori_loop(0, NZ, code, 0)
        for d in range(1, NZ):
            gz = (z + d) % NZ
            to = x * NZ + gz
            zcopies.append((
                start(send(zsnd.at[gz, at], zr.at[d - 1, at], zd_s.at[d - 1, k], zd_r.at[d - 1, k], to)),
                start(send(zscl.at[k], zs.at[d - 1, k], zc_s.at[d - 1, k], zc_r.at[d - 1, k], to)),
            ))

    pair(0)
    pair(1)
    neighbours(0)
    pair(2)
    neighbours(1)
    along_z(0)
    neighbours(2)

    @pl.when(chip < TILES)
    def _():
        pltpu.make_async_copy(st.at[c], st.at[c], s1_r).wait()

    st_copy = start(send(st.at[c], st.at[c], st_s, st_r, chip, 1 - c))
    along_z(1)

    st_copy.wait_recv()
    for a in range(3):
        mat[a, 456:480] = jnp.zeros((24, LANE), F32)
        new[a, 464:480] = jnp.zeros((16, LANE), F32)

    def place(s, i):
        i = jnp.minimum(i + (ob[i + 1] <= 4 * s).astype(I32), NODES - 1)
        offset = jnp.clip(4 * s - ob[i], 0, 4)
        for a in range(3):
            mat[a, pl.ds(4 * s, 4)] = st[i % 2, i // 2, a, pl.ds(offset, 4)]
        return i

    lax.fori_loop(0, SEGMENTS, place, jnp.int32(0))
    along_z(2)

    gcopies = []
    for k, (first, rows) in enumerate(CHUNKS):
        at = slice(first, first + rows)
        for pair_of in zcopies[7 * k : 7 * k + 7]:
            pair_of[0].wait_recv()
            pair_of[1].wait_recv()
        value = zsum[z, at]
        for d in range(NZ - 1):
            value = value + decode(zr[d, at], zs[d, k])
        both[c, at] = value
        gcopies.append(start(send(both.at[c, at], both.at[c, at], gc_s.at[k], gc_r.at[k], chip, 1 - c)))

    for copy in gcopies:
        copy.wait_recv()

    steps = step_count[0]
    rate = learning_rate[0]
    first_left = 1.0 - power(beta_first, steps)
    second_left = 1.0 - power(beta_second, steps)

    def step(half, begin, size):
        def body(b, carry):
            rows = pl.ds(pl.multiple_of(begin + b * size, 16), size)
            gradient = both[half, pl.ds(pl.multiple_of(b * size, 16), size)]
            master = mat[0, rows]
            first_new = beta_first * mat[1, rows] + (1.0 - beta_first) * gradient
            second_new = beta_second * mat[2, rows] + (1.0 - beta_second) * gradient * gradient
            first_hat = first_new / first_left
            second_hat = second_new / second_left
            new[0, rows] = master - rate * (first_hat / (jnp.sqrt(second_hat) + adam_eps) + decay * master)
            new[1, rows] = first_new
            new[2, rows] = second_new
            return carry

        return body

    lax.fori_loop(0, 7, step(0, 0, 32), 0)
    lax.fori_loop(0, 5, step(1, SECOND, 48), 0)

    for q in range(NY):
        wb[q] = new[0, 115 * q : 115 * q + 128].astype(BF16)
    mine = pl.ds(pl.multiple_of(c * PART, PART), PART)
    w1 = []
    for d in range(1, NY):
        to = (y + d) % NY
        w1.append(start(send(wb.at[to, mine], own.at[y], w1_s.at[d - 1], w1_r.at[d - 1], chip, to_y=to)))
    own[y] = wb[y, mine]

    def pick(m, carry):
        begin = jnp.clip(nb[2 * m + c], 0, UNITS)
        count = nb[2 * m + c + 1] - begin
        slot = lax.broadcasted_iota(I32, (CAP_NEW, LANE), 0)
        for a in range(3):
            rows = new[a, pl.ds(begin, CAP_NEW)]
            snd[m, CAP_NEW * a : CAP_NEW * (a + 1)] = jnp.where(slot < count, rows, 0.0)
        return carry

    lax.fori_loop(0, OWNERS // 2, pick, 0)

    for copy in w1:
        copy.wait_recv()
    keep = pltpu.make_async_copy(own, blocks.at[c, chip], own_s)
    keep.start()
    up, down = x * NZ + (z + 1) % NZ, x * NZ + (z + NZ - 1) % NZ
    right, left = ((x + 1) % NX) * NZ, ((x + 3) % NX) * NZ
    across = ((x + 2) % NX) * NZ
    from_left, from_right, relay_left, relay_right = [], [], [], []

    def share(src, slot, e):
        start(send(src, blocks.at[c, slot], cx_s.at[e], cx_r, chip, 1 - c))

    def climb(src, slot, s, part=None):
        dst = blocks.at[c, slot] if part is None else blocks.at[c, slot, part]
        return start(send(src, dst, zu_s.at[s], zu_r.at[s], up))

    def descend(src, slot, s, part=None):
        dst = blocks.at[c, slot] if part is None else blocks.at[c, slot, part]
        return start(send(src, dst, zd2_s.at[s], zd2_r.at[s], down))

    def spread(src, slot, e):
        from_left.append(start(send(src, blocks.at[c, slot], rt_s.at[e], rt_r.at[e], right + z)))
        from_right.append(start(send(src, blocks.at[c, slot], lf_s.at[e], lf_r.at[e], left + z)))
        share(src, slot, e)

    def relay(at, e):
        from_left[e].wait_recv()
        half = blocks.at[c, left + at, 0:2]
        relay_left.append(start(send(half, half, rr_s.at[e], rr_r.at[e], right + z)))
        share(blocks.at[c, left + at], left + at, 8 + e)
        from_right[e].wait_recv()
        half = blocks.at[c, right + at, 2:4]
        relay_right.append(start(send(half, half, rl_s.at[e], rl_r.at[e], left + z)))
        share(blocks.at[c, right + at], right + at, 16 + e)

    owner = (48 - c - chip) % CHIPS

    def owners_out(d, carry):
        to = (chip + d) % CHIPS
        m = (48 - c - to) % CHIPS

        @pl.when((m < OWNERS // 2) & (chip < TILES))
        def _():
            send(snd.at[m], r2.at[chip], s2_s, s2_r, to).start()

        return carry

    @pl.when((owner < OWNERS // 2) & (chip < TILES))
    def _():
        pltpu.make_async_copy(snd.at[owner], r2.at[chip], s2_r).start()

    place_of = [z]
    climbing, descending = climb(own, chip, 0), descend(own, chip, 0)
    spread(own, chip, 0)
    lax.fori_loop(1, 8, owners_out, 0)
    for s in range(1, NZ // 2):
        low, high = (z + NZ - s) % NZ, (z + s) % NZ
        climbing.wait_recv()
        block = blocks.at[c, x * NZ + low]
        if s < NZ // 2 - 1:
            climbing = climb(block, x * NZ + low, s)
        else:
            climbing = climb(blocks.at[c, x * NZ + low, 0:2], x * NZ + low, s, slice(0, 2))
        spread(block, x * NZ + low, 2 * s - 1)
        descending.wait_recv()
        block = blocks.at[c, x * NZ + high]
        if s < NZ // 2 - 1:
            descending = descend(block, x * NZ + high, s)
        else:
            descending = descend(blocks.at[c, x * NZ + high, 2:4], x * NZ + high, s, slice(2, 4))
        spread(block, x * NZ + high, 2 * s)
        for e in range(len(place_of) - (1 if s == 1 else 2), len(place_of)):
            relay(place_of[e], e)
        place_of += [low, high]
        lax.fori_loop(8 * s, 8 * s + 8, owners_out, 0)
    climbing.wait_recv()
    descending.wait_recv()
    last = (z + NZ // 2) % NZ
    spread(blocks.at[c, x * NZ + last], x * NZ + last, NZ - 1)
    place_of.append(last)

    for e in range(NZ - 3, NZ):
        relay(place_of[e], e)
    for e in range(NZ):
        relay_left[e].wait_recv()
        relay_right[e].wait_recv()
        slot = across + place_of[e]
        share(blocks.at[c, slot], slot, 24 + e)

    @pl.when(owner < OWNERS // 2)
    def _():
        pltpu.make_async_copy(r2.at[0:TILES], r2.at[0:TILES], s2_r).wait()

    @pl.when(owner >= OWNERS // 2)
    def _():
        zero[...] = jnp.zeros_like(zero)
        clear = pltpu.make_async_copy(zero, r2.at[0:TILES], s2_r)
        clear.start()
        clear.wait()

    @pl.when((owner < OWNERS // 2) & (chip < TILES))
    def _():
        pltpu.make_async_copy(snd.at[0:25], snd.at[0:25], s2_s).wait()

    @pl.when((owner >= OWNERS // 2) & (chip < TILES))
    def _():
        pltpu.make_async_copy(snd.at[0:26], snd.at[0:26], s2_s).wait()

    keep.wait()
    pltpu.make_async_copy(blocks.at[1 - c], blocks.at[1 - c], cx_r).wait()
    for k, (first, rows) in enumerate(CHUNKS):
        pltpu.make_async_copy(raw.at[first : first + rows], raw.at[first : first + rows], raw_s.at[k]).wait()

    @pl.when(chip < TILES)
    def _():
        pltpu.make_async_copy(stg.at[0:28], stg.at[0:28], s1_s).wait()

    @pl.when(chip >= TILES)
    def _():
        pltpu.make_async_copy(stg.at[0:29], stg.at[0:29], s1_s).wait()

    for copy in sent:
        copy.wait_send()


def lay_out(blocks, r2, o_m, o_f, o_s, o_w):
    q = pl.program_id(0)

    def tile(t, carry):
        for a, out in enumerate((o_m, o_f, o_s)):
            for s in range(CAP_NEW):
                out[s, t] = r2[t, CAP_NEW * a + s : CAP_NEW * a + s + 1]
        return carry

    lax.fori_loop(8 * q, jnp.minimum(8 * q + 8, TILES), tile, 0)
    for t in range(TILES):
        col = slice(t * LANE, (t + 1) * LANE)
        o_w[0:64, col] = blocks[0, t, 0]
        o_w[64:115, col] = blocks[1, t, 0, 0:51]


def on_device(grad_partials, old_master, old_first, old_second, old_bounds, new_bounds, step_count, learning_rate):
    smem = pl.BlockSpec(memory_space=pltpu.SMEM)
    dma = pltpu.SemaphoreType.DMA
    hbm = pl.BlockSpec(memory_space=pl.ANY)
    scale = pltpu.VMEM((NC, 1, LANE), F32)
    scratch = [
        pltpu.VMEM((HALF, WIDTH), BF16),
        pltpu.VMEM((HALF, WIDTH), BF16),
        pltpu.VMEM((16, WIDTH), BF16),
        pltpu.VMEM((3, 8, WIDTH), F32),
        pltpu.VMEM((CHIPS, HALF, LANE), F32),
        pltpu.VMEM((NZ, HALF, LANE), I16),
        pltpu.VMEM((NZ, HALF, LANE), I16),
        pltpu.VMEM((NZ, HALF, LANE), I16),
        scale, scale, scale,
        pltpu.VMEM((NZ // 2, HALF, LANE), I16),
        pltpu.VMEM((NZ // 2, HALF, LANE), I16),
        scale, scale,
        pltpu.VMEM((NZ, HALF, LANE), I16),
        pltpu.VMEM((NZ, HALF, LANE), I16),
        scale, scale,
        pltpu.VMEM((NZ, HALF, LANE), F32),
        pltpu.VMEM((NZ, HALF, LANE), I16),
        scale,
        pltpu.VMEM((NZ - 1, HALF, LANE), I16),
        pltpu.VMEM((NZ - 1, NC, 1, LANE), F32),
        pltpu.VMEM((2, HALF, LANE), F32),
        pltpu.VMEM((CHIPS, 3, 8, LANE), F32),
        pltpu.VMEM((2, CHIPS, 3, 8, LANE), F32),
        pltpu.VMEM((3, 480, LANE), F32),
        pltpu.VMEM((3, 480, LANE), F32),
        pltpu.VMEM((NY, 128, LANE), BF16),
        pltpu.VMEM((NY, PART, LANE), BF16),
        pltpu.VMEM((OWNERS // 2, 3 * CAP_NEW, LANE), F32),
        pltpu.VMEM((TILES, 3 * CAP_NEW, LANE), F32),
        dma((3,)), dma,
        dma((NC,)), dma((NC,)),
        dma((2, NC)), dma((2, NC)), dma((2, NC)), dma((2, NC)),
        dma((2, NC)), dma((2, NC)), dma((2, NC)), dma((2, NC)),
        dma((NZ - 1, NC)), dma((NZ - 1, NC)), dma((NZ - 1, NC)), dma((NZ - 1, NC)),
        dma((NC,)), dma((NC,)),
        dma, dma,
        dma, dma,
        dma((NY - 1,)), dma((NY - 1,)),
        dma((NZ // 2,)), dma((NZ // 2,)),
        dma((NZ // 2,)), dma((NZ // 2,)),
        dma((NZ,)), dma((NZ,)),
        dma((NZ,)), dma((NZ,)),
        dma((NZ,)), dma((NZ,)),
        dma((NZ,)), dma((NZ,)),
        dma((CHIPS,)), dma,
        dma, dma,
        dma,
    ]
    blocks, r2 = pl.pallas_call(
        kernel,
        name="adamw_move",
        out_shape=(
            jax.ShapeDtypeStruct((2, CHIPS, NY, PART, LANE), BF16),
            jax.ShapeDtypeStruct((CHIPS, 3 * CAP_NEW, LANE), F32),
        ),
        in_specs=[smem, smem, smem, smem, hbm, pl.BlockSpec((1, 16, WIDTH), lambda i: (0, 28, 0)), hbm, hbm, hbm],
        grid=(1,),
        out_specs=(hbm, hbm),
        scratch_shapes=scratch,
        compiler_params=pltpu.CompilerParams(collective_id=0, has_side_effects=True, vmem_limit_bytes=56 * 2**20),
    )(old_bounds, new_bounds, step_count, learning_rate, grad_partials, grad_partials, old_master, old_first, old_second)
    whole = pl.BlockSpec((CAP_NEW, TILES, 1, LANE), lambda q: (0, 0, 0, 0))
    rows = jax.ShapeDtypeStruct((CAP_NEW, TILES, 1, LANE), F32)
    outs = pl.pallas_call(
        lay_out,
        name="lay_out",
        grid=(NY,),
        out_shape=(rows, rows, rows, jax.ShapeDtypeStruct((115, NY * WIDTH), BF16)),
        in_specs=[
            pl.BlockSpec((2, CHIPS, 1, PART, LANE), lambda q: (0, 0, q, 0, 0)),
            pl.BlockSpec((CHIPS, 3 * CAP_NEW, LANE), lambda q: (0, 0, 0)),
        ],
        out_specs=(whole, whole, whole, pl.BlockSpec((115, WIDTH), lambda q: (0, q))),
    )(blocks, r2)
    return tuple(out.reshape(1, CAP_NEW, WIDTH) for out in outs[:3]) + (outs[3],)


def solution(mesh):
    split = P("node", None, "local")
    return jax.shard_map(
        on_device,
        mesh=mesh,
        in_specs=(split, split, split, split, P(), P(), P(), P()),
        out_specs=(split, split, split, P("local", None)),
        check_vma=False,
    )
```

```python
import jax
import jax.numpy as jnp
from jax import lax
from jax.experimental import pallas as pl
from jax.experimental.pallas import tpu as pltpu
from jax.sharding import PartitionSpec as P

MESH = pl.DeviceIdType.MESH
F32, BF16, I16, I32 = jnp.float32, jnp.bfloat16, jnp.int16, jnp.int32

UNITS = 460
WIDTH = 3712
LANE = 128
TILES = WIDTH // LANE
NODES = 64
CHIPS = 32
NX, NZ, NY = 4, 8, 4
HALF = 240
SECOND = 224
CHUNKS = ((0, 64), (64, 64), (128, 64), (192, 48))
NC = len(CHUNKS)
SEGMENTS = 115
CAP_NEW = 12
OWNERS = 52
PART = 64
LEVEL = 32760.0

beta_first = 0.9
beta_second = 0.95
adam_eps = 1e-08
decay = 0.1


def power(base, steps):
    result = jnp.float32(1.0)
    factor = float(base)
    for bit in range(5):
        result = jnp.where((steps // (1 << bit)) % 2 == 1, result * jnp.float32(factor), result)
        factor = factor * factor
    return result


def encode(value, inverse):
    return jnp.round(value * inverse).astype(I32).astype(I16)


def decode(code, scale):
    return code.astype(I32).astype(F32) * scale


def kernel(
    ob_in, nb_in, steps_in, rate_in, g, end, om, of, os_,
    blocks, r2,
    ob, nb, step_count, learning_rate,
    mine_g, raw, tail, olds, total, acode, right_code, left_code, scl, rscl, lscl,
    a_left, a_right, sa_left, sa_right, f_left, f_right, sf_left, sf_right,
    zsum, zsnd, zscl, zr, zs, both,
    stg, st, mat, new, wb, own, snd, zero,
    sc_s, col_s, in_s, own_g, raw_s, raw_r, a_s, a_r, as_s, as_r, f_s, f_r, fs_s, fs_r, zd_s, zd_r, zc_s, zc_r, gc_s, gc_r,
    s1_s, s1_r, st_s, st_r, w1_s, w1_r, zp_s, zp_r, zq_s, zq_r, xq_s, xq_r, rt_s, rt_r, lf_s, lf_r,
    rr_s, rr_r, rl_s, rl_r, cx_s, cx_r, s2_s, s2_r, own_s,
):
    node, y = lax.axis_index("node"), lax.axis_index("local")
    c, chip = node % 2, node // 2
    x, z = chip // NZ, chip % NZ

    def send(src, dst, ss, rs, to_chip, to_core=None, to_y=None):
        core = c if to_core is None else to_core
        return pltpu.make_async_remote_copy(
            src_ref=src, dst_ref=dst, send_sem=ss, recv_sem=rs,
            device_id=(to_chip * 2 + core, y if to_y is None else to_y), device_id_type=MESH,
        )

    sent = []

    def start(copy):
        copy.start()
        sent.append(copy)
        return copy

    barrier = pltpu.get_barrier_semaphore()

    def greet(to_chip, to_core, to_y):
        pl.semaphore_signal(barrier, inc=1, device_id=(to_chip * 2 + to_core, to_y), device_id_type=MESH)

    greet(chip, 1 - c, y)
    for d in range(1, NX):
        greet((x + d) % NX * NZ + z, c, y)
    for d in range(1, NZ):
        greet(x * NZ + (z + d) % NZ, c, y)
    for d in range(1, NY):
        greet(chip, c, (y + d) % NY)

    scalars = [
        pltpu.make_async_copy(src, dst, sc_s.at[a])
        for a, (src, dst) in enumerate(((ob_in, ob), (nb_in, nb), (steps_in, step_count), (rate_in, learning_rate)))
    ]
    for copy in scalars:
        copy.start()
    state_in = [pltpu.make_async_copy(old.at[0], olds.at[a], in_s.at[a]) for a, old in enumerate((om, of, os_))]
    for copy in state_in:
        copy.start()
    row = lax.broadcasted_iota(I32, (16, WIDTH), 0)
    tail[...] = jnp.where(row < 12, end[0].astype(F32), 0.0).astype(BF16)

    @pl.when(c == 0)
    def _():
        pltpu.make_async_copy(g.at[0, 0:HALF], mine_g, own_g).start()

    @pl.when(c == 1)
    def _():
        pltpu.make_async_copy(g.at[0, SECOND:448], mine_g.at[0:224], own_g).start()
        mine_g[224:240] = tail[...]

    for copy in state_in:
        copy.wait()

    def stage(t, carry):
        col = pl.ds(pl.multiple_of(t * LANE, LANE), LANE)
        for a in range(3):
            stg[t, a] = olds[a, :, col]
        return carry

    lax.fori_loop(0, TILES, stage, 0)
    for t in range(TILES, CHIPS):
        total[t] = jnp.zeros((HALF, LANE), F32)

    pl.semaphore_wait(barrier, 1 + NX - 1 + NZ - 1 + NY - 1)

    @pl.when(c == 0)
    def _():
        for k, (first, rows) in enumerate(CHUNKS):
            rows = min(rows, 224 - first)
            send(g.at[0, SECOND + first : SECOND + first + rows], raw.at[first : first + rows], raw_s.at[k], raw_r.at[k], chip, 1).start()
        send(tail, raw.at[224:240], raw_s.at[NC - 1], raw_r.at[NC - 1], chip, 1).start()

    @pl.when(c == 1)
    def _():
        for k, (first, rows) in enumerate(CHUNKS):
            send(g.at[0, first : first + rows], raw.at[first : first + rows], raw_s.at[k], raw_r.at[k], chip, 0).start()

    @pl.when(c == 0)
    def _():
        pltpu.make_async_copy(mine_g, mine_g, own_g).wait()

    @pl.when(c == 1)
    def _():
        pltpu.make_async_copy(mine_g.at[0:224], mine_g.at[0:224], own_g).wait()

    for d in range(1, NX):
        pl.semaphore_signal(col_s, inc=1, device_id=(((x + d) % NX * NZ + z) * 2 + c, y), device_id_type=MESH)

    right_x, left_x, far_x = (x + 1) % NX, (x + 3) % NX, (x + 2) % NX
    right_chip, left_chip = right_x * NZ + z, left_x * NZ + z
    acopies, fcopies, zcopies = [], [], []

    def pair(k):
        first, rows = CHUNKS[k]
        at = slice(first, first + rows)
        pltpu.make_async_copy(raw.at[at], raw.at[at], raw_r.at[k]).wait()

        def add(t, top):
            col = pl.ds(pl.multiple_of(t * LANE, LANE), LANE)
            value = mine_g[at, col].astype(F32) + raw[at, col].astype(F32)
            total[t, at] = value
            return jnp.maximum(top, jnp.abs(value))

        top = lax.fori_loop(0, TILES, add, jnp.zeros((rows, LANE), F32))
        top = jnp.maximum(jnp.max(top, axis=0, keepdims=True), 1e-30)
        scl[k] = top / LEVEL
        inverse = LEVEL / top

        def code(t, carry):
            acode[t, at] = encode(total[far_x * NZ + t, at], inverse)
            return carry

        lax.fori_loop(0, NZ, code, 0)
        acopies.append((
            start(send(acode.at[0:4, at], a_left.at[:, at], a_s.at[0, k], a_r.at[0, k], right_chip)),
            start(send(acode.at[4:8, at], a_right.at[:, at], a_s.at[1, k], a_r.at[1, k], left_chip)),
            start(send(scl.at[k], sa_left.at[k], as_s.at[0, k], as_r.at[0, k], right_chip)),
            start(send(scl.at[k], sa_right.at[k], as_s.at[1, k], as_r.at[1, k], left_chip)),
        ))

    def neighbours(k):
        first, rows = CHUNKS[k]
        at = slice(first, first + rows)
        for copy in acopies[k]:
            copy.wait_recv()
        rscl[k] = scl[k] + sa_left[k]
        lscl[k] = scl[k] + sa_right[k]
        to_right, to_left = 1.0 / rscl[k], 1.0 / lscl[k]

        def code(t, carry):
            through = decode(a_left[t, at], sa_left[k])
            right_code[t, at] = encode(total[right_x * NZ + t, at] + through, to_right)
            right_code[t + 4, at] = encode(total[right_x * NZ + t + 4, at], to_right)
            through = decode(a_right[t, at], sa_right[k])
            left_code[t, at] = encode(total[left_x * NZ + t, at], to_left)
            left_code[t + 4, at] = encode(total[left_x * NZ + t + 4, at] + through, to_left)
            return carry

        lax.fori_loop(0, 4, code, 0)
        fcopies.append((
            start(send(right_code.at[:, at], f_left.at[:, at], f_s.at[0, k], f_r.at[0, k], right_chip)),
            start(send(left_code.at[:, at], f_right.at[:, at], f_s.at[1, k], f_r.at[1, k], left_chip)),
            start(send(rscl.at[k], sf_left.at[k], fs_s.at[0, k], fs_r.at[0, k], right_chip)),
            start(send(lscl.at[k], sf_right.at[k], fs_s.at[1, k], fs_r.at[1, k], left_chip)),
        ))

    def along_z(k):
        first, rows = CHUNKS[k]
        at = slice(first, first + rows)
        for copy in fcopies[k]:
            copy.wait_recv()
        zscl[k] = scl[k] + sf_left[k] + sf_right[k]
        inverse = 1.0 / zscl[k]

        def code(t, carry):
            value = total[x * NZ + t, at] + decode(f_left[t, at], sf_left[k]) + decode(f_right[t, at], sf_right[k])
            zsum[t, at] = value
            zsnd[t, at] = encode(value, inverse)
            return carry

        lax.fori_loop(0, NZ, code, 0)
        for d in range(1, NZ):
            gz = (z + d) % NZ
            to = x * NZ + gz
            zcopies.append((
                start(send(zsnd.at[gz, at], zr.at[d - 1, at], zd_s.at[d - 1, k], zd_r.at[d - 1, k], to)),
                start(send(zscl.at[k], zs.at[d - 1, k], zc_s.at[d - 1, k], zc_r.at[d - 1, k], to)),
            ))

    pair(0)
    pair(1)
    neighbours(0)
    pair(2)
    neighbours(1)

    pl.semaphore_wait(col_s, NX - 1)

    def state_out(d, carry):
        to = (chip + d) % CHIPS

        @pl.when(to < TILES)
        def _():
            send(stg.at[to], st.at[c, chip], s1_s, s1_r, to).start()

        return carry

    lax.fori_loop(1, CHIPS, state_out, 0)

    @pl.when(chip < TILES)
    def _():
        pltpu.make_async_copy(stg.at[chip], st.at[c, chip], s1_r).start()

    along_z(0)
    pair(3)
    neighbours(2)
    along_z(1)
    neighbours(3)
    along_z(2)

    @pl.when(chip < TILES)
    def _():
        pltpu.make_async_copy(st.at[c], st.at[c], s1_r).wait()

    st_copy = start(send(st.at[c], st.at[c], st_s, st_r, chip, 1 - c))
    along_z(3)
    for copy in scalars:
        copy.wait()

    st_copy.wait_recv()
    for a in range(3):
        mat[a, 456:480] = jnp.zeros((24, LANE), F32)
        new[a, 464:480] = jnp.zeros((16, LANE), F32)

    def place(s, i):
        i = jnp.minimum(i + (ob[i + 1] <= 4 * s).astype(I32), NODES - 1)
        offset = jnp.clip(4 * s - ob[i], 0, 4)
        for a in range(3):
            mat[a, pl.ds(4 * s, 4)] = st[i % 2, i // 2, a, pl.ds(offset, 4)]
        return i

    lax.fori_loop(0, SEGMENTS, place, jnp.int32(0))

    gcopies = []
    for k, (first, rows) in enumerate(CHUNKS):
        at = slice(first, first + rows)
        for pair_of in zcopies[7 * k : 7 * k + 7]:
            pair_of[0].wait_recv()
            pair_of[1].wait_recv()
        value = zsum[z, at]
        for d in range(NZ - 1):
            value = value + decode(zr[d, at], zs[d, k])
        both[c, at] = value
        gcopies.append(start(send(both.at[c, at], both.at[c, at], gc_s.at[k], gc_r.at[k], chip, 1 - c)))

    for copy in gcopies:
        copy.wait_recv()

    steps = step_count[0]
    rate = learning_rate[0]
    first_left = 1.0 - power(beta_first, steps)
    second_left = 1.0 - power(beta_second, steps)

    def step(half, begin, size):
        def body(b, carry):
            rows = pl.ds(pl.multiple_of(begin + b * size, 16), size)
            gradient = both[half, pl.ds(pl.multiple_of(b * size, 16), size)]
            master = mat[0, rows]
            first_new = beta_first * mat[1, rows] + (1.0 - beta_first) * gradient
            second_new = beta_second * mat[2, rows] + (1.0 - beta_second) * gradient * gradient
            first_hat = first_new / first_left
            second_hat = second_new / second_left
            new[0, rows] = master - rate * (first_hat / (jnp.sqrt(second_hat) + adam_eps) + decay * master)
            new[1, rows] = first_new
            new[2, rows] = second_new
            return carry

        return body

    lax.fori_loop(0, 7, step(0, 0, 32), 0)
    lax.fori_loop(0, 5, step(1, SECOND, 48), 0)

    for q in range(NY):
        wb[q] = new[0, 115 * q : 115 * q + 128].astype(BF16)
    mine = pl.ds(pl.multiple_of(c * PART, PART), PART)
    w1 = []
    for d in range(1, NY):
        to = (y + d) % NY
        w1.append(start(send(wb.at[to, mine], own.at[y], w1_s.at[d - 1], w1_r.at[d - 1], chip, to_y=to)))
    own[y] = wb[y, mine]

    def pick(m, carry):
        begin = jnp.clip(nb[2 * m + c], 0, UNITS)
        count = nb[2 * m + c + 1] - begin
        slot = lax.broadcasted_iota(I32, (CAP_NEW, LANE), 0)
        for a in range(3):
            rows = new[a, pl.ds(begin, CAP_NEW)]
            snd[m, CAP_NEW * a : CAP_NEW * (a + 1)] = jnp.where(slot < count, rows, 0.0)
        return carry

    lax.fori_loop(0, OWNERS // 2, pick, 0)

    for copy in w1:
        copy.wait_recv()
    keep = pltpu.make_async_copy(own, blocks.at[c, x, z], own_s)
    keep.start()
    up, down = x * NZ + (z + 1) % NZ, x * NZ + (z + NZ - 1) % NZ
    three, low_rows, high_rows = slice(0, 3), slice(0, 32), slice(32, 64)
    from_left, from_right, relay_left, relay_right = [], [], [], []
    shares = []

    def share(src, dst):
        shares.append(start(send(src, dst, cx_s.at[len(shares)], cx_r, chip, 1 - c)))

    def pass_on(src, dst, sems, way, s):
        return start(send(src, dst, sems[0].at[way, s], sems[1].at[way, s], (up, down)[way]))

    def spread(src, at, e):
        dst = blocks.at[c, x, at, three]
        from_left.append(start(send(src, dst, rt_s.at[e], rt_r.at[e], right_chip)))
        from_right.append(start(send(src, dst, lf_s.at[e], lf_r.at[e], left_chip)))
        share(src, dst)

    def relay(at, e):
        from_left[e].wait_recv()
        half = blocks.at[c, left_x, at, three, low_rows]
        relay_left.append(start(send(half, half, rr_s.at[e], rr_r.at[e], right_chip)))
        whole = blocks.at[c, left_x, at, three]
        share(whole, whole)
        from_right[e].wait_recv()
        half = blocks.at[c, right_x, at, three, high_rows]
        relay_right.append(start(send(half, half, rl_s.at[e], rl_r.at[e], left_chip)))
        whole = blocks.at[c, right_x, at, three]
        share(whole, whole)

    owner = (48 - c - chip) % CHIPS

    def owners_out(d, carry):
        to = (chip + d) % CHIPS
        m = (48 - c - to) % CHIPS

        @pl.when((m < OWNERS // 2) & (chip < TILES))
        def _():
            send(snd.at[m], r2.at[chip], s2_s, s2_r, to).start()

        return carry

    @pl.when((owner < OWNERS // 2) & (chip < TILES))
    def _():
        pltpu.make_async_copy(snd.at[owner], r2.at[chip], s2_r).start()

    zp, zq = (zp_s, zp_r), (zq_s, zq_r)
    places = [z]
    climbing, descending = (pass_on(own.at[three], blocks.at[c, x, z, three], zp, way, 0) for way in range(2))
    quarters = []
    for d in range(1, NX):
        to = (x + d) % NX * NZ + z
        quarters.append(start(send(own.at[3], blocks.at[c, x, z, 3], xq_s.at[d - 1], xq_r.at[d - 1], to)))
    spread(own.at[three], z, 0)
    lax.fori_loop(1, 8, owners_out, 0)
    keep.wait()
    for copy in quarters:
        copy.wait_recv()
    column = blocks.at[c, :, z, 3]
    rising, sinking = (pass_on(column, column, zq, way, 0) for way in range(2))
    share(column, column)
    for s in range(1, NZ // 2):
        low, high = (z + NZ - s) % NZ, (z + s) % NZ
        final = s == NZ // 2 - 1
        climbing.wait_recv()
        block = blocks.at[c, x, low, three]
        onward = blocks.at[c, x, low, three, low_rows] if final else block
        climbing = pass_on(onward, onward, zp, 0, s)
        spread(block, low, 2 * s - 1)
        descending.wait_recv()
        block = blocks.at[c, x, high, three]
        onward = blocks.at[c, x, high, three, high_rows] if final else block
        descending = pass_on(onward, onward, zp, 1, s)
        spread(block, high, 2 * s)
        rising.wait_recv()
        column = blocks.at[c, :, low, 3]
        onward = blocks.at[c, 0:2, low, 3] if final else column
        rising = pass_on(onward, onward, zq, 0, s)
        share(column, column)
        sinking.wait_recv()
        column = blocks.at[c, :, high, 3]
        onward = blocks.at[c, 2:4, high, 3] if final else column
        sinking = pass_on(onward, onward, zq, 1, s)
        share(column, column)
        for e in range(max(0, 2 * s - 3), 2 * s - 1):
            relay(places[e], e)
        places += [low, high]
        lax.fori_loop(8 * s, 8 * s + 8, owners_out, 0)
    climbing.wait_recv()
    descending.wait_recv()
    last = (z + NZ // 2) % NZ
    spread(blocks.at[c, x, last, three], last, NZ - 1)
    places.append(last)
    rising.wait_recv()
    sinking.wait_recv()
    column = blocks.at[c, :, last, 3]
    share(column, column)

    for e in range(NZ - 3, NZ):
        relay(places[e], e)

    for e in range(NZ):
        relay_left[e].wait_recv()
        relay_right[e].wait_recv()
        whole = blocks.at[c, far_x, places[e], three]
        share(whole, whole)

    @pl.when(owner < OWNERS // 2)
    def _():
        pltpu.make_async_copy(r2.at[0:TILES], r2.at[0:TILES], s2_r).wait()

    @pl.when(owner >= OWNERS // 2)
    def _():
        zero[...] = jnp.zeros_like(zero)
        clear = pltpu.make_async_copy(zero, r2.at[0:TILES], s2_r)
        clear.start()
        clear.wait()

    @pl.when((owner < OWNERS // 2) & (chip < TILES))
    def _():
        pltpu.make_async_copy(snd.at[0:25], snd.at[0:25], s2_s).wait()

    @pl.when((owner >= OWNERS // 2) & (chip < TILES))
    def _():
        pltpu.make_async_copy(snd.at[0:26], snd.at[0:26], s2_s).wait()

    pltpu.make_async_copy(blocks.at[1 - c], blocks.at[1 - c], cx_r).wait()
    for k, (first, rows) in enumerate(CHUNKS):
        pltpu.make_async_copy(raw.at[first : first + rows], raw.at[first : first + rows], raw_s.at[k]).wait()

    @pl.when(chip < TILES)
    def _():
        pltpu.make_async_copy(stg.at[0:28], stg.at[0:28], s1_s).wait()

    @pl.when(chip >= TILES)
    def _():
        pltpu.make_async_copy(stg.at[0:29], stg.at[0:29], s1_s).wait()

    for copy in sent:
        copy.wait_send()


def lay_out(blocks, r2, o_m, o_f, o_s, o_w, got, rows, state, wide, in_s, out_s):
    copies = [pltpu.make_async_copy(blocks.at[:, :, :, q], got.at[q], in_s.at[q]) for q in range(NY)]
    copies.append(pltpu.make_async_copy(r2, rows, in_s.at[NY]))
    for copy in copies:
        copy.start()
    outs = []

    def out(src, dst):
        outs.append(pltpu.make_async_copy(src, dst, out_s.at[len(outs)]))
        outs[-1].start()

    for q in range(NY):
        copies[q].wait()
        for t in range(TILES):
            col = slice(t * LANE, (t + 1) * LANE)
            wide[q, 0:64, col] = got[q, 0, t // NZ, t % NZ]
            wide[q, 64:115, col] = got[q, 1, t // NZ, t % NZ, 0:51]
        out(wide.at[q], o_w.at[:, q * WIDTH : (q + 1) * WIDTH])

    copies[NY].wait()

    def tile(t, carry):
        for a in range(3):
            for s in range(CAP_NEW):
                state[a, s, t] = rows[t, CAP_NEW * a + s : CAP_NEW * a + s + 1]
        return carry

    lax.fori_loop(0, TILES, tile, 0)
    for a, dst in enumerate((o_m, o_f, o_s)):
        out(state.at[a], dst)
    for copy in outs:
        copy.wait()


def on_device(grad_partials, old_master, old_first, old_second, old_bounds, new_bounds, step_count, learning_rate):
    dma = pltpu.SemaphoreType.DMA
    hbm = pl.BlockSpec(memory_space=pl.ANY)
    scale = pltpu.VMEM((NC, 1, LANE), F32)
    scratch = [
        pltpu.SMEM((NODES + 1,), I32),
        pltpu.SMEM((OWNERS + 1,), I32),
        pltpu.SMEM((1,), I32),
        pltpu.SMEM((1,), F32),
        pltpu.VMEM((HALF, WIDTH), BF16),
        pltpu.VMEM((HALF, WIDTH), BF16),
        pltpu.VMEM((16, WIDTH), BF16),
        pltpu.VMEM((3, 8, WIDTH), F32),
        pltpu.VMEM((CHIPS, HALF, LANE), F32),
        pltpu.VMEM((NZ, HALF, LANE), I16),
        pltpu.VMEM((NZ, HALF, LANE), I16),
        pltpu.VMEM((NZ, HALF, LANE), I16),
        scale, scale, scale,
        pltpu.VMEM((NZ // 2, HALF, LANE), I16),
        pltpu.VMEM((NZ // 2, HALF, LANE), I16),
        scale, scale,
        pltpu.VMEM((NZ, HALF, LANE), I16),
        pltpu.VMEM((NZ, HALF, LANE), I16),
        scale, scale,
        pltpu.VMEM((NZ, HALF, LANE), F32),
        pltpu.VMEM((NZ, HALF, LANE), I16),
        scale,
        pltpu.VMEM((NZ - 1, HALF, LANE), I16),
        pltpu.VMEM((NZ - 1, NC, 1, LANE), F32),
        pltpu.VMEM((2, HALF, LANE), F32),
        pltpu.VMEM((CHIPS, 3, 8, LANE), F32),
        pltpu.VMEM((2, CHIPS, 3, 8, LANE), F32),
        pltpu.VMEM((3, 480, LANE), F32),
        pltpu.VMEM((3, 480, LANE), F32),
        pltpu.VMEM((NY, 128, LANE), BF16),
        pltpu.VMEM((NY, PART, LANE), BF16),
        pltpu.VMEM((OWNERS // 2, 3 * CAP_NEW, LANE), F32),
        pltpu.VMEM((TILES, 3 * CAP_NEW, LANE), F32),
        dma((4,)), pltpu.SemaphoreType.REGULAR,
        dma((3,)), dma,
        dma((NC,)), dma((NC,)),
        dma((2, NC)), dma((2, NC)), dma((2, NC)), dma((2, NC)),
        dma((2, NC)), dma((2, NC)), dma((2, NC)), dma((2, NC)),
        dma((NZ - 1, NC)), dma((NZ - 1, NC)), dma((NZ - 1, NC)), dma((NZ - 1, NC)),
        dma((NC,)), dma((NC,)),
        dma, dma,
        dma, dma,
        dma((NY - 1,)), dma((NY - 1,)),
        dma((2, NZ // 2)), dma((2, NZ // 2)),
        dma((2, NZ // 2)), dma((2, NZ // 2)),
        dma((NX - 1,)), dma((NX - 1,)),
        dma((NZ,)), dma((NZ,)),
        dma((NZ,)), dma((NZ,)),
        dma((NZ,)), dma((NZ,)),
        dma((NZ,)), dma((NZ,)),
        dma((40,)), dma,
        dma, dma,
        dma,
    ]
    blocks, r2 = pl.pallas_call(
        kernel,
        name="adamw_move",
        out_shape=(
            jax.ShapeDtypeStruct((2, NX, NZ, NY, PART, LANE), BF16),
            jax.ShapeDtypeStruct((CHIPS, 3 * CAP_NEW, LANE), F32),
        ),
        in_specs=[hbm, hbm, hbm, hbm, hbm, pl.BlockSpec((1, 16, WIDTH), lambda i: (0, 28, 0)), hbm, hbm, hbm],
        grid=(1,),
        out_specs=(hbm, hbm),
        scratch_shapes=scratch,
        compiler_params=pltpu.CompilerParams(collective_id=0, has_side_effects=True, vmem_limit_bytes=56 * 2**20),
    )(old_bounds, new_bounds, step_count, learning_rate, grad_partials, grad_partials, old_master, old_first, old_second)
    rows = jax.ShapeDtypeStruct((CAP_NEW, TILES, 1, LANE), F32)
    outs = pl.pallas_call(
        lay_out,
        name="lay_out",
        out_shape=(rows, rows, rows, jax.ShapeDtypeStruct((115, NY * WIDTH), BF16)),
        in_specs=[hbm, hbm],
        out_specs=(hbm, hbm, hbm, hbm),
        scratch_shapes=[
            pltpu.VMEM((NY, 2, NX, NZ, PART, LANE), BF16),
            pltpu.VMEM((CHIPS, 3 * CAP_NEW, LANE), F32),
            pltpu.VMEM((3, CAP_NEW, TILES, 1, LANE), F32),
            pltpu.VMEM((NY, 115, WIDTH), BF16),
            dma((NY + 1,)),
            dma((NY + 3,)),
        ],
        compiler_params=pltpu.CompilerParams(vmem_limit_bytes=60 * 2**20),
    )(blocks, r2)
    return tuple(out.reshape(1, CAP_NEW, WIDTH) for out in outs[:3]) + (outs[3],)


def solution(mesh):
    split = P("node", None, "local")
    return jax.shard_map(
        on_device,
        mesh=mesh,
        in_specs=(split, split, split, split, P(), P(), P(), P()),
        out_specs=(split, split, split, P("local", None)),
        check_vma=False,
    )
```

```python
import jax
import jax.numpy as jnp
from jax import lax
from jax.experimental import pallas as pl
from jax.experimental.pallas import tpu as pltpu
from jax.sharding import PartitionSpec as P

MESH = pl.DeviceIdType.MESH
F32, BF16, I16, I32 = jnp.float32, jnp.bfloat16, jnp.int16, jnp.int32

UNITS = 460
WIDTH = 3712
LANE = 128
TILES = WIDTH // LANE
NODES = 64
CHIPS = 32
NX, NZ, NY = 4, 8, 4
HALF = 240
SECOND = 224
CHUNKS = ((0, 64), (64, 64), (128, 64), (192, 48))
NC = len(CHUNKS)
SEGMENTS = 115
CAP_NEW = 12
OWNERS = 52
PART = 64
LEVEL = 32760.0

beta_first = 0.9
beta_second = 0.95
adam_eps = 1e-08
decay = 0.1


def power(base, steps):
    result = jnp.float32(1.0)
    factor = float(base)
    for bit in range(5):
        result = jnp.where((steps // (1 << bit)) % 2 == 1, result * jnp.float32(factor), result)
        factor = factor * factor
    return result


def encode(value, inverse):
    return jnp.round(value * inverse).astype(I32).astype(I16)


def decode(code, scale):
    return code.astype(I32).astype(F32) * scale


def kernel(
    ob_in, nb_in, steps_in, rate_in, g, end, om, of, os_,
    blocks, r2,
    ob, nb, step_count, learning_rate,
    mine_g, raw, tail, olds, total, acode, right_code, left_code, scl, rscl, lscl, a_in, sa, f_in, sf,
    zsum, zsnd, zscl, zr, zs, grad,
    stg, st, mat, new, peer, wb, snd, zero,
    sc_s, col_s, in_s, own_g, raw_s, raw_r, a_s, a_r, as_s, as_r, f_s, f_r, fs_s, fs_r, zd_s, zd_r, zc_s, zc_r,
    s1_s, s1_r, st_s, st_r, ex_s, ex_r, w_s, w_r, x_s, x_r, far_s, far_r, cx_s, cx_r, s2_s, s2_r,
):
    node, y = lax.axis_index("node"), lax.axis_index("local")
    c, chip = node % 2, node // 2
    x, z = chip // NZ, chip % NZ

    def send(src, dst, ss, rs, to_chip, to_core=None, to_y=None):
        core = c if to_core is None else to_core
        return pltpu.make_async_remote_copy(
            src_ref=src, dst_ref=dst, send_sem=ss, recv_sem=rs,
            device_id=(to_chip * 2 + core, y if to_y is None else to_y), device_id_type=MESH,
        )

    def start(src, dst, ss, rs, to_chip, to_core=None, to_y=None):
        send(src, dst, ss, rs, to_chip, to_core, to_y).start()

    def arrived(ref, sem):
        pltpu.make_async_copy(ref, ref, sem).wait()

    barrier = pltpu.get_barrier_semaphore()

    def greet(to_chip, to_core, to_y):
        pl.semaphore_signal(barrier, inc=1, device_id=(to_chip * 2 + to_core, to_y), device_id_type=MESH)

    greet(chip, 1 - c, y)
    for d in range(1, NX):
        greet((x + d) % NX * NZ + z, c, y)
    for d in range(1, NZ):
        greet(x * NZ + (z + d) % NZ, c, y)
    for d in range(1, NY):
        greet(chip, c, (y + d) % NY)

    scalars = [
        pltpu.make_async_copy(src, dst, sc_s.at[a])
        for a, (src, dst) in enumerate(((ob_in, ob), (nb_in, nb), (steps_in, step_count), (rate_in, learning_rate)))
    ]
    for copy in scalars:
        copy.start()
    state_in = [pltpu.make_async_copy(old.at[0], olds.at[a], in_s.at[a]) for a, old in enumerate((om, of, os_))]
    for copy in state_in:
        copy.start()
    row = lax.broadcasted_iota(I32, (16, WIDTH), 0)
    tail[...] = jnp.where(row < 12, end[0].astype(F32), 0.0).astype(BF16)

    @pl.when(c == 0)
    def _():
        pltpu.make_async_copy(g.at[0, 0:HALF], mine_g, own_g).start()

    @pl.when(c == 1)
    def _():
        pltpu.make_async_copy(g.at[0, SECOND:448], mine_g.at[0:224], own_g).start()
        mine_g[224:240] = tail[...]

    for copy in state_in:
        copy.wait()

    def stage(t, carry):
        col = pl.ds(pl.multiple_of(t * LANE, LANE), LANE)
        for a in range(3):
            stg[t, a] = olds[a, :, col]
        return carry

    lax.fori_loop(0, TILES, stage, 0)
    for t in range(TILES, CHIPS):
        total[t] = jnp.zeros((HALF, LANE), F32)

    pl.semaphore_wait(barrier, 1 + NX - 1 + NZ - 1 + NY - 1)

    @pl.when(c == 0)
    def _():
        for k, (first, rows) in enumerate(CHUNKS):
            rows = min(rows, 224 - first)
            send(g.at[0, SECOND + first : SECOND + first + rows], raw.at[first : first + rows], raw_s.at[k], raw_r.at[k], chip, 1).start()
        send(tail, raw.at[224:240], raw_s.at[NC - 1], raw_r.at[NC - 1], chip, 1).start()

    @pl.when(c == 1)
    def _():
        for k, (first, rows) in enumerate(CHUNKS):
            send(g.at[0, first : first + rows], raw.at[first : first + rows], raw_s.at[k], raw_r.at[k], chip, 0).start()

    @pl.when(c == 0)
    def _():
        pltpu.make_async_copy(mine_g, mine_g, own_g).wait()

    @pl.when(c == 1)
    def _():
        pltpu.make_async_copy(mine_g.at[0:224], mine_g.at[0:224], own_g).wait()

    for d in range(1, NX):
        pl.semaphore_signal(col_s, inc=1, device_id=(((x + d) % NX * NZ + z) * 2 + c, y), device_id_type=MESH)

    right_x, left_x, far_x = (x + 1) % NX, (x + 3) % NX, (x + 2) % NX
    right_chip, left_chip = right_x * NZ + z, left_x * NZ + z

    def pair(k):
        first, rows = CHUNKS[k]
        at = slice(first, first + rows)
        arrived(raw.at[at], raw_r.at[k])

        def add(t, top):
            col = pl.ds(pl.multiple_of(t * LANE, LANE), LANE)
            value = mine_g[at, col].astype(F32) + raw[at, col].astype(F32)
            total[t, at] = value
            return jnp.maximum(top, jnp.abs(value))

        top = lax.fori_loop(0, TILES, add, jnp.zeros((rows, LANE), F32))
        top = jnp.maximum(jnp.max(top, axis=0, keepdims=True), 1e-30)
        scl[k] = top / LEVEL
        inverse = LEVEL / top

        def code(t, carry):
            acode[t, at] = encode(total[far_x * NZ + t, at], inverse)
            return carry

        lax.fori_loop(0, NZ, code, 0)
        start(acode.at[0:4, at], a_in.at[0, :, at], a_s, a_r.at[k], right_chip)
        start(acode.at[4:8, at], a_in.at[1, :, at], a_s, a_r.at[k], left_chip)
        start(scl.at[k], sa.at[0, k], as_s, as_r.at[k], right_chip)
        start(scl.at[k], sa.at[1, k], as_s, as_r.at[k], left_chip)

    def neighbours(k):
        first, rows = CHUNKS[k]
        at = slice(first, first + rows)
        arrived(a_in.at[:, :, at], a_r.at[k])
        arrived(sa.at[:, k], as_r.at[k])
        rscl[k] = scl[k] + sa[0, k]
        lscl[k] = scl[k] + sa[1, k]
        to_right, to_left = 1.0 / rscl[k], 1.0 / lscl[k]

        def code(t, carry):
            through = decode(a_in[0, t, at], sa[0, k])
            right_code[t, at] = encode(total[right_x * NZ + t, at] + through, to_right)
            right_code[t + 4, at] = encode(total[right_x * NZ + t + 4, at], to_right)
            through = decode(a_in[1, t, at], sa[1, k])
            left_code[t, at] = encode(total[left_x * NZ + t, at], to_left)
            left_code[t + 4, at] = encode(total[left_x * NZ + t + 4, at] + through, to_left)
            return carry

        lax.fori_loop(0, 4, code, 0)
        start(right_code.at[:, at], f_in.at[0, :, at], f_s, f_r.at[k], right_chip)
        start(left_code.at[:, at], f_in.at[1, :, at], f_s, f_r.at[k], left_chip)
        start(rscl.at[k], sf.at[0, k], fs_s, fs_r.at[k], right_chip)
        start(lscl.at[k], sf.at[1, k], fs_s, fs_r.at[k], left_chip)

    def along_z(k):
        first, rows = CHUNKS[k]
        at = slice(first, first + rows)
        arrived(f_in.at[:, :, at], f_r.at[k])
        arrived(sf.at[:, k], fs_r.at[k])
        zscl[k] = scl[k] + sf[0, k] + sf[1, k]
        inverse = 1.0 / zscl[k]

        def code(t, carry):
            value = total[x * NZ + t, at] + decode(f_in[0, t, at], sf[0, k]) + decode(f_in[1, t, at], sf[1, k])
            zsum[t, at] = value
            zsnd[t, at] = encode(value, inverse)
            return carry

        lax.fori_loop(0, NZ, code, 0)
        for d in range(1, NZ):
            gz = (z + d) % NZ
            to = x * NZ + gz
            start(zsnd.at[gz, at], zr.at[d - 1, at], zd_s, zd_r.at[k], to)
            start(zscl.at[k], zs.at[d - 1, k], zc_s, zc_r.at[k], to)

    pair(0)
    pair(1)
    neighbours(0)
    pair(2)
    neighbours(1)

    pl.semaphore_wait(col_s, NX - 1)

    def state_out(d, carry):
        to = (chip + d) % CHIPS

        @pl.when(to < TILES)
        def _():
            send(stg.at[to], st.at[c, chip], s1_s, s1_r, to).start()

        return carry

    lax.fori_loop(1, CHIPS, state_out, 0)

    @pl.when(chip < TILES)
    def _():
        pltpu.make_async_copy(stg.at[chip], st.at[c, chip], s1_r).start()

    along_z(0)
    pair(3)
    neighbours(2)
    along_z(1)
    neighbours(3)
    along_z(2)

    @pl.when(chip < TILES)
    def _():
        arrived(st.at[c], s1_r)

    start(st.at[c], st.at[c], st_s, st_r, chip, 1 - c)
    along_z(3)
    for copy in scalars:
        copy.wait()

    arrived(st.at[1 - c], st_r)
    for a in range(3):
        new[a, 464:480] = jnp.zeros((16, LANE), F32)

    def owner_of(s, i):
        return jnp.minimum(i + (ob[i + 1] <= 4 * s).astype(I32), NODES - 1)

    def place(s, i):
        i = owner_of(s, i)
        offset = jnp.clip(4 * s - ob[i], 0, 4)
        for a in range(3):
            mat[a, pl.ds(4 * s, 4)] = st[i % 2, i // 2, a, pl.ds(offset, 4)]
        return i

    before = lax.fori_loop(0, c * (SECOND // 4), owner_of, jnp.int32(0))
    lax.fori_loop(c * (SECOND // 4), c * (SECOND // 4) + HALF // 4, place, before)

    for k, (first, rows) in enumerate(CHUNKS):
        at = slice(first, first + rows)
        arrived(zr.at[:, at], zd_r.at[k])
        arrived(zs.at[:, k], zc_r.at[k])
        value = zsum[z, at]
        for d in range(NZ - 1):
            value = value + decode(zr[d, at], zs[d, k])
        grad[at] = value

    steps = step_count[0]
    rate = learning_rate[0]
    first_left = 1.0 - power(beta_first, steps)
    second_left = 1.0 - power(beta_second, steps)

    def step(b, carry):
        rows = pl.ds(pl.multiple_of(c * SECOND + b * 48, 16), 48)
        gradient = grad[pl.ds(pl.multiple_of(b * 48, 16), 48)]
        master = mat[0, rows]
        first_new = beta_first * mat[1, rows] + (1.0 - beta_first) * gradient
        second_new = beta_second * mat[2, rows] + (1.0 - beta_second) * gradient * gradient
        first_hat = first_new / first_left
        second_hat = second_new / second_left
        new[0, rows] = master - rate * (first_hat / (jnp.sqrt(second_hat) + adam_eps) + decay * master)
        new[1, rows] = first_new
        new[2, rows] = second_new
        return carry

    lax.fori_loop(0, HALF // 48, step, 0)

    for i in range(2):
        rows = new[0, pl.ds(c * 230 + 115 * i, 120)]
        wb[i] = jnp.concatenate([rows, jnp.zeros((8, LANE), F32)], axis=0).astype(BF16)
    for dz in (0, 4, 1, 7, 2, 6, 3, 5):
        for i in range(2):
            yy = 2 * c + i
            to = x * NZ + (z + dz) % NZ
            for other in range(2):
                core = (c + other) % 2
                src = wb.at[i, pl.ds(pl.multiple_of(core * PART, PART), PART)]
                dst = blocks.at[core, x, z, y]
                if dz == 0 and other == 0:
                    @pl.when(yy == y)
                    def _():
                        pltpu.make_async_copy(src, dst, w_r.at[0]).start()

                    @pl.when(yy != y)
                    def _():
                        start(src, dst, w_s, w_r.at[0], to, core, yy)
                else:
                    start(src, dst, w_s, w_r.at[dz], to, core, yy)

    @pl.when(c == 0)
    def _():
        send(new.at[:, 0:224], peer, ex_s, ex_r, chip, 1).start()

    @pl.when(c == 1)
    def _():
        send(new.at[:, 240:464], peer, ex_s, ex_r, chip, 0).start()

    arrived(peer, ex_r)
    theirs = pl.ds(pl.multiple_of((1 - c) * HALF, 16), 224)
    for a in range(3):
        new[a, theirs] = peer[a]

    def pick(m, carry):
        begin = jnp.clip(nb[2 * m + c], 0, UNITS)
        count = nb[2 * m + c + 1] - begin
        slot = lax.broadcasted_iota(I32, (CAP_NEW, LANE), 0)
        for a in range(3):
            rows = new[a, pl.ds(begin, CAP_NEW)]
            snd[m, CAP_NEW * a : CAP_NEW * (a + 1)] = jnp.where(slot < count, rows, 0.0)
        return carry

    lax.fori_loop(0, OWNERS // 2, pick, 0)

    def share(ref):
        start(ref, ref, cx_s, cx_r, chip, 1 - c)

    def spread(at, e):
        ref = blocks.at[c, x, at]
        start(ref, ref, x_s, x_r.at[0, e], right_chip)
        start(ref, ref, x_s, x_r.at[1, e], left_chip)
        share(ref)

    def relay(at, e):
        arrived(blocks.at[c, left_x, at], x_r.at[0, e])
        half = blocks.at[c, left_x, at, 0:2]
        start(half, half, far_s, far_r.at[e], right_chip)
        arrived(blocks.at[c, right_x, at], x_r.at[1, e])
        half = blocks.at[c, right_x, at, 2:4]
        start(half, half, far_s, far_r.at[e], left_chip)
        share(blocks.at[c, left_x, at])
        share(blocks.at[c, right_x, at])

    owner = (48 - c - chip) % CHIPS

    def owners_out(d, carry):
        to = (chip + d) % CHIPS
        m = (48 - c - to) % CHIPS

        @pl.when((m < OWNERS // 2) & (chip < TILES))
        def _():
            send(snd.at[m], r2.at[chip], s2_s, s2_r, to).start()

        return carry

    @pl.when((owner < OWNERS // 2) & (chip < TILES))
    def _():
        pltpu.make_async_copy(snd.at[owner], r2.at[chip], s2_r).start()

    order = (0, 1, 7, 2, 6, 3, 5, 4)
    for n, dz in enumerate(order):
        at = (z + NZ - dz) % NZ
        arrived(blocks.at[c, x, at], w_r.at[dz])
        spread(at, dz)
        if n >= 2:
            relay((z + NZ - order[n - 2]) % NZ, order[n - 2])
        if n >= 4:
            lax.fori_loop(max(8 * (n - 4), 1), 8 * (n - 4) + 8, owners_out, 0)

    for dz in order[6:]:
        relay((z + NZ - dz) % NZ, dz)

    for dz in order:
        ref = blocks.at[c, far_x, (z + NZ - dz) % NZ]
        arrived(ref, far_r.at[dz])
        share(ref)

    @pl.when(owner < OWNERS // 2)
    def _():
        arrived(r2.at[0:TILES], s2_r)

    @pl.when(owner >= OWNERS // 2)
    def _():
        zero[...] = jnp.zeros_like(zero)
        clear = pltpu.make_async_copy(zero, r2.at[0:TILES], s2_r)
        clear.start()
        clear.wait()

    @pl.when((owner < OWNERS // 2) & (chip < TILES))
    def _():
        arrived(snd.at[0:25], s2_s)

    @pl.when((owner >= OWNERS // 2) & (chip < TILES))
    def _():
        arrived(snd.at[0:26], s2_s)

    arrived(blocks.at[1 - c], cx_r)
    for k, (first, rows) in enumerate(CHUNKS):
        arrived(raw.at[first : first + rows], raw_s.at[k])

    @pl.when(chip < TILES)
    def _():
        arrived(stg.at[0:28], s1_s)

    @pl.when(chip >= TILES)
    def _():
        arrived(stg.at[0:29], s1_s)

    @pl.when(y // 2 != c)
    def _():
        arrived(blocks.at[c, 0], w_s)

    @pl.when(y // 2 == c)
    def _():
        arrived(total.at[0:31, 0:32], w_s)

    for ref, sem in (
        (acode, a_s), (sa, as_s), (f_in, f_s), (sf, fs_s), (zr, zd_s), (zs, zc_s), (st.at[c], st_s),
        (peer, ex_s), (blocks.at[c, 0:2], x_s), (blocks.at[c, 0], far_s), (blocks.at[c], cx_s),
    ):
        arrived(ref, sem)


def lay_out(blocks, r2, o_m, o_f, o_s, o_w, got, rows, state, wide, in_s, out_s):
    copies = [pltpu.make_async_copy(blocks.at[:, :, :, q], got.at[q], in_s.at[q]) for q in range(NY)]
    copies.append(pltpu.make_async_copy(r2, rows, in_s.at[NY]))
    for copy in copies:
        copy.start()
    outs = []

    def out(src, dst):
        outs.append(pltpu.make_async_copy(src, dst, out_s.at[len(outs)]))
        outs[-1].start()

    for q in range(NY):
        copies[q].wait()
        for t in range(TILES):
            col = slice(t * LANE, (t + 1) * LANE)
            wide[q, 0:64, col] = got[q, 0, t // NZ, t % NZ]
            wide[q, 64:115, col] = got[q, 1, t // NZ, t % NZ, 0:51]
        out(wide.at[q], o_w.at[:, q * WIDTH : (q + 1) * WIDTH])

    copies[NY].wait()

    def tile(t, carry):
        for a in range(3):
            for s in range(CAP_NEW):
                state[a, s, t] = rows[t, CAP_NEW * a + s : CAP_NEW * a + s + 1]
        return carry

    lax.fori_loop(0, TILES, tile, 0)
    for a, dst in enumerate((o_m, o_f, o_s)):
        out(state.at[a], dst)
    for copy in outs:
        copy.wait()


def on_device(grad_partials, old_master, old_first, old_second, old_bounds, new_bounds, step_count, learning_rate):
    dma = pltpu.SemaphoreType.DMA
    hbm = pl.BlockSpec(memory_space=pl.ANY)
    scale = pltpu.VMEM((NC, 1, LANE), F32)
    scratch = [
        pltpu.SMEM((NODES + 1,), I32),
        pltpu.SMEM((OWNERS + 1,), I32),
        pltpu.SMEM((1,), I32),
        pltpu.SMEM((1,), F32),
        pltpu.VMEM((HALF, WIDTH), BF16),
        pltpu.VMEM((HALF, WIDTH), BF16),
        pltpu.VMEM((16, WIDTH), BF16),
        pltpu.VMEM((3, 8, WIDTH), F32),
        pltpu.VMEM((CHIPS, HALF, LANE), F32),
        pltpu.VMEM((NZ, HALF, LANE), I16),
        pltpu.VMEM((NZ, HALF, LANE), I16),
        pltpu.VMEM((NZ, HALF, LANE), I16),
        scale, scale, scale,
        pltpu.VMEM((2, NZ // 2, HALF, LANE), I16),
        pltpu.VMEM((2, NC, 1, LANE), F32),
        pltpu.VMEM((2, NZ, HALF, LANE), I16),
        pltpu.VMEM((2, NC, 1, LANE), F32),
        pltpu.VMEM((NZ, HALF, LANE), F32),
        pltpu.VMEM((NZ, HALF, LANE), I16),
        scale,
        pltpu.VMEM((NZ - 1, HALF, LANE), I16),
        pltpu.VMEM((NZ - 1, NC, 1, LANE), F32),
        pltpu.VMEM((HALF, LANE), F32),
        pltpu.VMEM((CHIPS, 3, 8, LANE), F32),
        pltpu.VMEM((2, CHIPS, 3, 8, LANE), F32),
        pltpu.VMEM((3, 480, LANE), F32),
        pltpu.VMEM((3, 480, LANE), F32),
        pltpu.VMEM((3, 224, LANE), F32),
        pltpu.VMEM((2, 128, LANE), BF16),
        pltpu.VMEM((OWNERS // 2, 3 * CAP_NEW, LANE), F32),
        pltpu.VMEM((TILES, 3 * CAP_NEW, LANE), F32),
        dma((4,)), pltpu.SemaphoreType.REGULAR,
        dma((3,)), dma,
        dma((NC,)), dma((NC,)),
        dma, dma((NC,)), dma, dma((NC,)), dma, dma((NC,)), dma, dma((NC,)),
        dma, dma((NC,)), dma, dma((NC,)),
        dma, dma, dma, dma, dma, dma,
        dma, dma((NZ,)), dma, dma((2, NZ)), dma, dma((NZ,)), dma, dma,
        dma, dma,
    ]
    blocks, r2 = pl.pallas_call(
        kernel,
        name="adamw_move",
        out_shape=(
            jax.ShapeDtypeStruct((2, NX, NZ, NY, PART, LANE), BF16),
            jax.ShapeDtypeStruct((CHIPS, 3 * CAP_NEW, LANE), F32),
        ),
        in_specs=[hbm, hbm, hbm, hbm, hbm, pl.BlockSpec((1, 16, WIDTH), lambda i: (0, 28, 0)), hbm, hbm, hbm],
        grid=(1,),
        out_specs=(hbm, hbm),
        scratch_shapes=scratch,
        compiler_params=pltpu.CompilerParams(collective_id=0, has_side_effects=True, vmem_limit_bytes=56 * 2**20),
    )(old_bounds, new_bounds, step_count, learning_rate, grad_partials, grad_partials, old_master, old_first, old_second)
    rows = jax.ShapeDtypeStruct((CAP_NEW, TILES, 1, LANE), F32)
    outs = pl.pallas_call(
        lay_out,
        name="lay_out",
        out_shape=(rows, rows, rows, jax.ShapeDtypeStruct((115, NY * WIDTH), BF16)),
        in_specs=[hbm, hbm],
        out_specs=(hbm, hbm, hbm, hbm),
        scratch_shapes=[
            pltpu.VMEM((NY, 2, NX, NZ, PART, LANE), BF16),
            pltpu.VMEM((CHIPS, 3 * CAP_NEW, LANE), F32),
            pltpu.VMEM((3, CAP_NEW, TILES, 1, LANE), F32),
            pltpu.VMEM((NY, 115, WIDTH), BF16),
            dma((NY + 1,)),
            dma((NY + 3,)),
        ],
        compiler_params=pltpu.CompilerParams(vmem_limit_bytes=60 * 2**20),
    )(blocks, r2)
    return tuple(out.reshape(1, CAP_NEW, WIDTH) for out in outs[:3]) + (outs[3],)


def solution(mesh):
    split = P("node", None, "local")
    return jax.shard_map(
        on_device,
        mesh=mesh,
        in_specs=(split, split, split, split, P(), P(), P(), P()),
        out_specs=(split, split, split, P("local", None)),
        check_vma=False,
    )
```

```python
import jax
import jax.numpy as jnp
from jax import lax
from jax.experimental import pallas as pl
from jax.experimental.pallas import tpu as pltpu
from jax.sharding import PartitionSpec as P

MESH = pl.DeviceIdType.MESH
F32, BF16, I16, I32 = jnp.float32, jnp.bfloat16, jnp.int16, jnp.int32

UNITS = 460
WIDTH = 3712
LANE = 128
TILES = WIDTH // LANE
NODES = 64
CHIPS = 32
NX, NZ, NY = 4, 8, 4
HALF = 240
SECOND = 224
CHUNKS = ((0, 64), (64, 64), (128, 64), (192, 48))
NC = len(CHUNKS)
SEGMENTS = 115
CAP_NEW = 12
OWNERS = 52
PART = 64
LEVEL = 32760.0

beta_first = 0.9
beta_second = 0.95
adam_eps = 1e-08
decay = 0.1


def power(base, steps):
    result = jnp.float32(1.0)
    factor = float(base)
    for bit in range(5):
        result = jnp.where((steps // (1 << bit)) % 2 == 1, result * jnp.float32(factor), result)
        factor = factor * factor
    return result


def encode(value, inverse):
    return jnp.round(value * inverse).astype(I32).astype(I16)


def decode(code, scale):
    return code.astype(I32).astype(F32) * scale


def kernel(
    ob_in, nb_in, steps_in, rate_in, g, end, om, of, os_,
    blocks, r2,
    ob, nb, step_count, learning_rate,
    mine_g, raw, tail, olds, total, acode, right_code, left_code, scl, rscl, lscl, a_in, sa, f_in, sf,
    zsum, zsnd, zscl, zr, zs, grad,
    stg, st, mat, new, peer, wb, snd, zero,
    sc_s, col_s, in_s, own_g, raw_s, raw_r, a_s, a_r, as_s, as_r, f_s, f_r, fs_s, fs_r, zd_s, zd_r, zc_s, zc_r,
    s1_s, s1_r, st_s, st_r, ex_s, ex_r, w_s, w_r, x_s, x_r, far_s, far_r, cx_s, cx_r, s2_s, s2_r,
):
    node, y = lax.axis_index("node"), lax.axis_index("local")
    c, chip = node % 2, node // 2
    x, z = chip // NZ, chip % NZ

    def send(src, dst, ss, rs, to_chip, to_core=None, to_y=None):
        core = c if to_core is None else to_core
        return pltpu.make_async_remote_copy(
            src_ref=src, dst_ref=dst, send_sem=ss, recv_sem=rs,
            device_id=(to_chip * 2 + core, y if to_y is None else to_y), device_id_type=MESH,
        )

    def start(src, dst, ss, rs, to_chip, to_core=None, to_y=None):
        send(src, dst, ss, rs, to_chip, to_core, to_y).start()

    def arrived(ref, sem):
        pltpu.make_async_copy(ref, ref, sem).wait()

    barrier = pltpu.get_barrier_semaphore()

    def greet(to_chip, to_core, to_y):
        pl.semaphore_signal(barrier, inc=1, device_id=(to_chip * 2 + to_core, to_y), device_id_type=MESH)

    greet(chip, 1 - c, y)
    for d in range(1, NX):
        greet((x + d) % NX * NZ + z, c, y)
    for d in range(1, NZ):
        greet(x * NZ + (z + d) % NZ, c, y)
    for d in range(1, NY):
        greet(chip, c, (y + d) % NY)

    scalars = [
        pltpu.make_async_copy(src, dst, sc_s.at[a])
        for a, (src, dst) in enumerate(((ob_in, ob), (nb_in, nb), (steps_in, step_count), (rate_in, learning_rate)))
    ]
    for copy in scalars:
        copy.start()
    state_in = [pltpu.make_async_copy(old.at[0], olds.at[a], in_s.at[a]) for a, old in enumerate((om, of, os_))]
    for copy in state_in:
        copy.start()
    row = lax.broadcasted_iota(I32, (16, WIDTH), 0)
    tail[...] = jnp.where(row < 12, end[0].astype(F32), 0.0).astype(BF16)

    @pl.when(c == 0)
    def _():
        pltpu.make_async_copy(g.at[0, 0:HALF], mine_g, own_g).start()

    @pl.when(c == 1)
    def _():
        pltpu.make_async_copy(g.at[0, SECOND:448], mine_g.at[0:224], own_g).start()
        mine_g[224:240] = tail[...]

    for copy in state_in:
        copy.wait()

    def stage(t, carry):
        col = pl.ds(pl.multiple_of(t * LANE, LANE), LANE)
        for a in range(3):
            stg[t, a] = olds[a, :, col]
        return carry

    lax.fori_loop(0, TILES, stage, 0)
    for t in range(TILES, CHIPS):
        total[t] = jnp.zeros((HALF, LANE), F32)

    pl.semaphore_wait(barrier, 1 + NX - 1 + NZ - 1 + NY - 1)

    @pl.when(c == 0)
    def _():
        for k, (first, rows) in enumerate(CHUNKS):
            rows = min(rows, 224 - first)
            send(g.at[0, SECOND + first : SECOND + first + rows], raw.at[first : first + rows], raw_s.at[k], raw_r.at[k], chip, 1).start()
        send(tail, raw.at[224:240], raw_s.at[NC - 1], raw_r.at[NC - 1], chip, 1).start()

    @pl.when(c == 1)
    def _():
        for k, (first, rows) in enumerate(CHUNKS):
            send(g.at[0, first : first + rows], raw.at[first : first + rows], raw_s.at[k], raw_r.at[k], chip, 0).start()

    @pl.when(c == 0)
    def _():
        pltpu.make_async_copy(mine_g, mine_g, own_g).wait()

    @pl.when(c == 1)
    def _():
        pltpu.make_async_copy(mine_g.at[0:224], mine_g.at[0:224], own_g).wait()

    for d in range(1, NX):
        pl.semaphore_signal(col_s, inc=1, device_id=(((x + d) % NX * NZ + z) * 2 + c, y), device_id_type=MESH)

    right_x, left_x, far_x = (x + 1) % NX, (x + 3) % NX, (x + 2) % NX
    right_chip, left_chip = right_x * NZ + z, left_x * NZ + z

    def pair(k):
        first, rows = CHUNKS[k]
        at = slice(first, first + rows)
        arrived(raw.at[at], raw_r.at[k])

        def add(t, top):
            col = pl.ds(pl.multiple_of(t * LANE, LANE), LANE)
            value = mine_g[at, col].astype(F32) + raw[at, col].astype(F32)
            total[t, at] = value
            return jnp.maximum(top, jnp.abs(value))

        top = lax.fori_loop(0, TILES, add, jnp.zeros((rows, LANE), F32))
        top = jnp.maximum(jnp.max(top, axis=0, keepdims=True), 1e-30)
        scl[k] = top / LEVEL
        inverse = LEVEL / top

        def code(t, carry):
            acode[t, at] = encode(total[far_x * NZ + t, at], inverse)
            return carry

        lax.fori_loop(0, NZ, code, 0)
        start(acode.at[0:4, at], a_in.at[0, :, at], a_s, a_r.at[k], right_chip)
        start(acode.at[4:8, at], a_in.at[1, :, at], a_s, a_r.at[k], left_chip)
        start(scl.at[k], sa.at[0, k], as_s, as_r.at[k], right_chip)
        start(scl.at[k], sa.at[1, k], as_s, as_r.at[k], left_chip)

    def neighbours(k):
        first, rows = CHUNKS[k]
        at = slice(first, first + rows)
        arrived(a_in.at[:, :, at], a_r.at[k])
        arrived(sa.at[:, k], as_r.at[k])
        rscl[k] = scl[k] + sa[0, k]
        lscl[k] = scl[k] + sa[1, k]
        to_right, to_left = 1.0 / rscl[k], 1.0 / lscl[k]

        def code(t, carry):
            through = decode(a_in[0, t, at], sa[0, k])
            right_code[t, at] = encode(total[right_x * NZ + t, at] + through, to_right)
            right_code[t + 4, at] = encode(total[right_x * NZ + t + 4, at], to_right)
            through = decode(a_in[1, t, at], sa[1, k])
            left_code[t, at] = encode(total[left_x * NZ + t, at], to_left)
            left_code[t + 4, at] = encode(total[left_x * NZ + t + 4, at] + through, to_left)
            return carry

        lax.fori_loop(0, 4, code, 0)
        start(right_code.at[:, at], f_in.at[0, :, at], f_s, f_r.at[k], right_chip)
        start(left_code.at[:, at], f_in.at[1, :, at], f_s, f_r.at[k], left_chip)
        start(rscl.at[k], sf.at[0, k], fs_s, fs_r.at[k], right_chip)
        start(lscl.at[k], sf.at[1, k], fs_s, fs_r.at[k], left_chip)

    def along_z(k):
        first, rows = CHUNKS[k]
        at = slice(first, first + rows)
        arrived(f_in.at[:, :, at], f_r.at[k])
        arrived(sf.at[:, k], fs_r.at[k])
        zscl[k] = scl[k] + sf[0, k] + sf[1, k]
        inverse = 1.0 / zscl[k]

        def code(t, carry):
            value = total[x * NZ + t, at] + decode(f_in[0, t, at], sf[0, k]) + decode(f_in[1, t, at], sf[1, k])
            zsum[t, at] = value
            zsnd[t, at] = encode(value, inverse)
            return carry

        lax.fori_loop(0, NZ, code, 0)
        for d in range(1, NZ):
            gz = (z + d) % NZ
            to = x * NZ + gz
            start(zsnd.at[gz, at], zr.at[d - 1, at], zd_s, zd_r.at[k], to)
            start(zscl.at[k], zs.at[d - 1, k], zc_s, zc_r.at[k], to)

    pair(0)
    pair(1)
    neighbours(0)
    pair(2)
    neighbours(1)

    pl.semaphore_wait(col_s, NX - 1)

    def state_out(d, carry):
        to = (chip + d) % CHIPS

        @pl.when(to < TILES)
        def _():
            send(stg.at[to], st.at[c, chip], s1_s, s1_r, to).start()

        return carry

    lax.fori_loop(1, CHIPS, state_out, 0)

    @pl.when(chip < TILES)
    def _():
        pltpu.make_async_copy(stg.at[chip], st.at[c, chip], s1_r).start()

    along_z(0)
    pair(3)
    neighbours(2)
    along_z(1)
    neighbours(3)
    along_z(2)

    @pl.when(chip < TILES)
    def _():
        arrived(st.at[c], s1_r)

    start(st.at[c], st.at[c], st_s, st_r, chip, 1 - c)
    along_z(3)
    for copy in scalars:
        copy.wait()

    arrived(st.at[1 - c], st_r)
    for a in range(3):
        new[a, 464:480] = jnp.zeros((16, LANE), F32)

    def owner_of(s, i):
        return jnp.minimum(i + (ob[i + 1] <= 4 * s).astype(I32), NODES - 1)

    def place(s, i):
        i = owner_of(s, i)
        offset = jnp.clip(4 * s - ob[i], 0, 4)
        for a in range(3):
            mat[a, pl.ds(4 * s, 4)] = st[i % 2, i // 2, a, pl.ds(offset, 4)]
        return i

    before = lax.fori_loop(0, c * (SECOND // 4), owner_of, jnp.int32(0))
    lax.fori_loop(c * (SECOND // 4), c * (SECOND // 4) + HALF // 4, place, before)

    for k, (first, rows) in enumerate(CHUNKS):
        at = slice(first, first + rows)
        arrived(zr.at[:, at], zd_r.at[k])
        arrived(zs.at[:, k], zc_r.at[k])
        value = zsum[z, at]
        for d in range(NZ - 1):
            value = value + decode(zr[d, at], zs[d, k])
        grad[at] = value

    steps = step_count[0]
    rate = learning_rate[0]
    first_left = 1.0 - power(beta_first, steps)
    second_left = 1.0 - power(beta_second, steps)

    def step(b, carry):
        rows = pl.ds(pl.multiple_of(c * SECOND + b * 48, 16), 48)
        gradient = grad[pl.ds(pl.multiple_of(b * 48, 16), 48)]
        master = mat[0, rows]
        first_new = beta_first * mat[1, rows] + (1.0 - beta_first) * gradient
        second_new = beta_second * mat[2, rows] + (1.0 - beta_second) * gradient * gradient
        first_hat = first_new / first_left
        second_hat = second_new / second_left
        new[0, rows] = master - rate * (first_hat / (jnp.sqrt(second_hat) + adam_eps) + decay * master)
        new[1, rows] = first_new
        new[2, rows] = second_new
        return carry

    lax.fori_loop(0, HALF // 48, step, 0)

    for i in range(2):
        rows = new[0, pl.ds(c * 230 + 115 * i, 120)]
        wb[i] = jnp.concatenate([rows, jnp.zeros((8, LANE), F32)], axis=0).astype(BF16)
    for dz in (0, 4, 1, 7, 2, 6, 3, 5):
        for i in range(2):
            yy = 2 * c + i
            to = x * NZ + (z + dz) % NZ
            for other in range(2):
                core = (c + other) % 2
                src = wb.at[i, pl.ds(pl.multiple_of(core * PART, PART), PART)]
                dst = blocks.at[core, x, z, y]
                if dz == 0 and other == 0:
                    @pl.when(yy == y)
                    def _():
                        pltpu.make_async_copy(src, dst, w_r.at[0]).start()

                    @pl.when(yy != y)
                    def _():
                        start(src, dst, w_s, w_r.at[0], to, core, yy)
                else:
                    start(src, dst, w_s, w_r.at[dz], to, core, yy)

    @pl.when(c == 0)
    def _():
        send(new.at[:, 0:224], peer, ex_s, ex_r, chip, 1).start()

    @pl.when(c == 1)
    def _():
        send(new.at[:, 240:464], peer, ex_s, ex_r, chip, 0).start()

    arrived(peer, ex_r)
    theirs = pl.ds(pl.multiple_of((1 - c) * HALF, 16), 224)
    for a in range(3):
        new[a, theirs] = peer[a]

    def pick(m, carry):
        begin = jnp.clip(nb[2 * m + c], 0, UNITS)
        count = nb[2 * m + c + 1] - begin
        slot = lax.broadcasted_iota(I32, (CAP_NEW, LANE), 0)
        for a in range(3):
            rows = new[a, pl.ds(begin, CAP_NEW)]
            snd[m, CAP_NEW * a : CAP_NEW * (a + 1)] = jnp.where(slot < count, rows, 0.0)
        return carry

    lax.fori_loop(0, OWNERS // 2, pick, 0)

    def share(ref):
        start(ref, ref, cx_s, cx_r, chip, 1 - c)

    def spread(at, e):
        ref = blocks.at[c, x, at]
        start(ref, ref, x_s, x_r.at[0, e], right_chip)
        start(ref, ref, x_s, x_r.at[1, e], left_chip)
        share(ref)

    def relay(at, e):
        arrived(blocks.at[c, left_x, at], x_r.at[0, e])
        half = blocks.at[c, left_x, at, 0:2]
        start(half, half, far_s, far_r.at[e], right_chip)
        arrived(blocks.at[c, right_x, at], x_r.at[1, e])
        half = blocks.at[c, right_x, at, 2:4]
        start(half, half, far_s, far_r.at[e], left_chip)
        share(blocks.at[c, left_x, at])
        share(blocks.at[c, right_x, at])

    owner = (48 - c - chip) % CHIPS

    def owners_out(d, carry):
        to = (chip + d) % CHIPS
        m = (48 - c - to) % CHIPS

        @pl.when((m < OWNERS // 2) & (chip < TILES))
        def _():
            send(snd.at[m], r2.at[chip], s2_s, s2_r, to).start()

        return carry

    @pl.when((owner < OWNERS // 2) & (chip < TILES))
    def _():
        pltpu.make_async_copy(snd.at[owner], r2.at[chip], s2_r).start()

    order = (0, 1, 7, 2, 6, 3, 5, 4)
    for n, dz in enumerate(order):
        at = (z + NZ - dz) % NZ
        arrived(blocks.at[c, x, at], w_r.at[dz])
        spread(at, dz)
        if n >= 2:
            relay((z + NZ - order[n - 2]) % NZ, order[n - 2])
        if n == 0:
            lax.fori_loop(1, 32, owners_out, 0)

    for dz in order[6:]:
        relay((z + NZ - dz) % NZ, dz)

    for dz in order:
        ref = blocks.at[c, far_x, (z + NZ - dz) % NZ]
        arrived(ref, far_r.at[dz])
        share(ref)

    @pl.when(owner < OWNERS // 2)
    def _():
        arrived(r2.at[0:TILES], s2_r)

    @pl.when(owner >= OWNERS // 2)
    def _():
        zero[...] = jnp.zeros_like(zero)
        clear = pltpu.make_async_copy(zero, r2.at[0:TILES], s2_r)
        clear.start()
        clear.wait()

    @pl.when((owner < OWNERS // 2) & (chip < TILES))
    def _():
        arrived(snd.at[0:25], s2_s)

    @pl.when((owner >= OWNERS // 2) & (chip < TILES))
    def _():
        arrived(snd.at[0:26], s2_s)

    arrived(blocks.at[1 - c], cx_r)
    for k, (first, rows) in enumerate(CHUNKS):
        arrived(raw.at[first : first + rows], raw_s.at[k])

    @pl.when(chip < TILES)
    def _():
        arrived(stg.at[0:28], s1_s)

    @pl.when(chip >= TILES)
    def _():
        arrived(stg.at[0:29], s1_s)

    @pl.when(y // 2 != c)
    def _():
        arrived(blocks.at[c, 0], w_s)

    @pl.when(y // 2 == c)
    def _():
        arrived(total.at[0:31, 0:32], w_s)

    for ref, sem in (
        (acode, a_s), (sa, as_s), (f_in, f_s), (sf, fs_s), (zr, zd_s), (zs, zc_s), (st.at[c], st_s),
        (peer, ex_s), (blocks.at[c, 0:2], x_s), (blocks.at[c, 0], far_s), (blocks.at[c], cx_s),
    ):
        arrived(ref, sem)


def lay_out(blocks, r2, o_m, o_f, o_s, o_w, got, rows, state, wide, in_s, out_s):
    copies = [pltpu.make_async_copy(blocks.at[:, :, :, q], got.at[q], in_s.at[q]) for q in range(NY)]
    copies.append(pltpu.make_async_copy(r2, rows, in_s.at[NY]))
    for copy in copies:
        copy.start()
    outs = []

    def out(src, dst):
        outs.append(pltpu.make_async_copy(src, dst, out_s.at[len(outs)]))
        outs[-1].start()

    for q in range(NY):
        copies[q].wait()
        for t in range(TILES):
            col = slice(t * LANE, (t + 1) * LANE)
            wide[q, 0:64, col] = got[q, 0, t // NZ, t % NZ]
            wide[q, 64:115, col] = got[q, 1, t // NZ, t % NZ, 0:51]
        out(wide.at[q], o_w.at[:, q * WIDTH : (q + 1) * WIDTH])

    copies[NY].wait()

    def tile(t, carry):
        for a in range(3):
            for s in range(CAP_NEW):
                state[a, s, t] = rows[t, CAP_NEW * a + s : CAP_NEW * a + s + 1]
        return carry

    lax.fori_loop(0, TILES, tile, 0)
    for a, dst in enumerate((o_m, o_f, o_s)):
        out(state.at[a], dst)
    for copy in outs:
        copy.wait()


def on_device(grad_partials, old_master, old_first, old_second, old_bounds, new_bounds, step_count, learning_rate):
    dma = pltpu.SemaphoreType.DMA
    hbm = pl.BlockSpec(memory_space=pl.ANY)
    scale = pltpu.VMEM((NC, 1, LANE), F32)
    scratch = [
        pltpu.SMEM((NODES + 1,), I32),
        pltpu.SMEM((OWNERS + 1,), I32),
        pltpu.SMEM((1,), I32),
        pltpu.SMEM((1,), F32),
        pltpu.VMEM((HALF, WIDTH), BF16),
        pltpu.VMEM((HALF, WIDTH), BF16),
        pltpu.VMEM((16, WIDTH), BF16),
        pltpu.VMEM((3, 8, WIDTH), F32),
        pltpu.VMEM((CHIPS, HALF, LANE), F32),
        pltpu.VMEM((NZ, HALF, LANE), I16),
        pltpu.VMEM((NZ, HALF, LANE), I16),
        pltpu.VMEM((NZ, HALF, LANE), I16),
        scale, scale, scale,
        pltpu.VMEM((2, NZ // 2, HALF, LANE), I16),
        pltpu.VMEM((2, NC, 1, LANE), F32),
        pltpu.VMEM((2, NZ, HALF, LANE), I16),
        pltpu.VMEM((2, NC, 1, LANE), F32),
        pltpu.VMEM((NZ, HALF, LANE), F32),
        pltpu.VMEM((NZ, HALF, LANE), I16),
        scale,
        pltpu.VMEM((NZ - 1, HALF, LANE), I16),
        pltpu.VMEM((NZ - 1, NC, 1, LANE), F32),
        pltpu.VMEM((HALF, LANE), F32),
        pltpu.VMEM((CHIPS, 3, 8, LANE), F32),
        pltpu.VMEM((2, CHIPS, 3, 8, LANE), F32),
        pltpu.VMEM((3, 480, LANE), F32),
        pltpu.VMEM((3, 480, LANE), F32),
        pltpu.VMEM((3, 224, LANE), F32),
        pltpu.VMEM((2, 128, LANE), BF16),
        pltpu.VMEM((OWNERS // 2, 3 * CAP_NEW, LANE), F32),
        pltpu.VMEM((TILES, 3 * CAP_NEW, LANE), F32),
        dma((4,)), pltpu.SemaphoreType.REGULAR,
        dma((3,)), dma,
        dma((NC,)), dma((NC,)),
        dma, dma((NC,)), dma, dma((NC,)), dma, dma((NC,)), dma, dma((NC,)),
        dma, dma((NC,)), dma, dma((NC,)),
        dma, dma, dma, dma, dma, dma,
        dma, dma((NZ,)), dma, dma((2, NZ)), dma, dma((NZ,)), dma, dma,
        dma, dma,
    ]
    blocks, r2 = pl.pallas_call(
        kernel,
        name="adamw_move",
        out_shape=(
            jax.ShapeDtypeStruct((2, NX, NZ, NY, PART, LANE), BF16),
            jax.ShapeDtypeStruct((CHIPS, 3 * CAP_NEW, LANE), F32),
        ),
        in_specs=[hbm, hbm, hbm, hbm, hbm, pl.BlockSpec((1, 16, WIDTH), lambda i: (0, 28, 0)), hbm, hbm, hbm],
        grid=(1,),
        out_specs=(hbm, hbm),
        scratch_shapes=scratch,
        compiler_params=pltpu.CompilerParams(collective_id=0, has_side_effects=True, vmem_limit_bytes=56 * 2**20),
    )(old_bounds, new_bounds, step_count, learning_rate, grad_partials, grad_partials, old_master, old_first, old_second)
    rows = jax.ShapeDtypeStruct((CAP_NEW, TILES, 1, LANE), F32)
    outs = pl.pallas_call(
        lay_out,
        name="lay_out",
        out_shape=(rows, rows, rows, jax.ShapeDtypeStruct((115, NY * WIDTH), BF16)),
        in_specs=[hbm, hbm],
        out_specs=(hbm, hbm, hbm, hbm),
        scratch_shapes=[
            pltpu.VMEM((NY, 2, NX, NZ, PART, LANE), BF16),
            pltpu.VMEM((CHIPS, 3 * CAP_NEW, LANE), F32),
            pltpu.VMEM((3, CAP_NEW, TILES, 1, LANE), F32),
            pltpu.VMEM((NY, 115, WIDTH), BF16),
            dma((NY + 1,)),
            dma((NY + 3,)),
        ],
        compiler_params=pltpu.CompilerParams(vmem_limit_bytes=60 * 2**20),
    )(blocks, r2)
    return tuple(out.reshape(1, CAP_NEW, WIDTH) for out in outs[:3]) + (outs[3],)


def solution(mesh):
    split = P("node", None, "local")
    return jax.shard_map(
        on_device,
        mesh=mesh,
        in_specs=(split, split, split, split, P(), P(), P(), P()),
        out_specs=(split, split, split, P("local", None)),
        check_vma=False,
    )
```

```python
import jax
import jax.numpy as jnp
from jax import lax
from jax.experimental import pallas as pl
from jax.experimental.pallas import tpu as pltpu
from jax.sharding import PartitionSpec as P

MESH = pl.DeviceIdType.MESH
F32, BF16, I16, I32 = jnp.float32, jnp.bfloat16, jnp.int16, jnp.int32

UNITS = 460
WIDTH = 3712
LANE = 128
TILES = WIDTH // LANE
NODES = 64
CHIPS = 32
NX, NZ, NY = 4, 8, 4
HALF = 240
SECOND = 224
CHUNKS = ((0, 64), (64, 64), (128, 64), (192, 48))
NC = len(CHUNKS)
SEGMENTS = 115
CAP_NEW = 12
OWNERS = 52
PART = 64
LEVEL = 32760.0

beta_first = 0.9
beta_second = 0.95
adam_eps = 1e-08
decay = 0.1


def power(base, steps):
    result = jnp.float32(1.0)
    factor = float(base)
    for bit in range(5):
        result = jnp.where((steps // (1 << bit)) % 2 == 1, result * jnp.float32(factor), result)
        factor = factor * factor
    return result


def encode(value, inverse):
    return jnp.round(value * inverse).astype(I32).astype(I16)


def decode(code, scale):
    return code.astype(I32).astype(F32) * scale


def kernel(
    ob_in, nb_in, steps_in, rate_in, g, end, om, of, os_,
    blocks, r2,
    ob, nb, step_count, learning_rate,
    mine_g, raw, tail, olds, total, acode, right_code, left_code, scl, rscl, lscl, a_in, sa, f_in, sf,
    zsum, zsnd, zscl, zr, zs, grad,
    stg, st, mat, new, peer, wb, snd, zero,
    sc_s, col_s, in_s, own_g, raw_s, raw_r, a_s, a_r, as_s, as_r, f_s, f_r, fs_s, fs_r, zd_s, zd_r, zc_s, zc_r,
    s1_s, s1_r, st_s, st_r, ex_s, ex_r, w_s, w_r, x_s, x_r, far_s, far_r, cx_s, cx_r, s2_s, s2_r,
):
    node, y = lax.axis_index("node"), lax.axis_index("local")
    c, chip = node % 2, node // 2
    x, z = chip // NZ, chip % NZ

    def send(src, dst, ss, rs, to_chip, to_core=None, to_y=None):
        core = c if to_core is None else to_core
        return pltpu.make_async_remote_copy(
            src_ref=src, dst_ref=dst, send_sem=ss, recv_sem=rs,
            device_id=(to_chip * 2 + core, y if to_y is None else to_y), device_id_type=MESH,
        )

    def start(src, dst, ss, rs, to_chip, to_core=None, to_y=None):
        send(src, dst, ss, rs, to_chip, to_core, to_y).start()

    def arrived(ref, sem):
        pltpu.make_async_copy(ref, ref, sem).wait()

    barrier = pltpu.get_barrier_semaphore()

    def greet(to_chip, to_core, to_y):
        pl.semaphore_signal(barrier, inc=1, device_id=(to_chip * 2 + to_core, to_y), device_id_type=MESH)

    greet(chip, 1 - c, y)
    for d in range(1, NX):
        greet((x + d) % NX * NZ + z, c, y)
    for d in range(1, NZ):
        greet(x * NZ + (z + d) % NZ, c, y)
    for d in range(1, NY):
        greet(chip, c, (y + d) % NY)

    scalars = [
        pltpu.make_async_copy(src, dst, sc_s.at[a])
        for a, (src, dst) in enumerate(((ob_in, ob), (nb_in, nb), (steps_in, step_count), (rate_in, learning_rate)))
    ]
    for copy in scalars:
        copy.start()
    state_in = [pltpu.make_async_copy(old.at[0], olds.at[a], in_s.at[a]) for a, old in enumerate((om, of, os_))]
    for copy in state_in:
        copy.start()
    row = lax.broadcasted_iota(I32, (16, WIDTH), 0)
    tail[...] = jnp.where(row < 12, end[0].astype(F32), 0.0).astype(BF16)

    @pl.when(c == 0)
    def _():
        pltpu.make_async_copy(g.at[0, 0:HALF], mine_g, own_g).start()

    @pl.when(c == 1)
    def _():
        pltpu.make_async_copy(g.at[0, SECOND:448], mine_g.at[0:224], own_g).start()
        mine_g[224:240] = tail[...]

    for copy in state_in:
        copy.wait()

    def stage(t, carry):
        col = pl.ds(pl.multiple_of(t * LANE, LANE), LANE)
        for a in range(3):
            stg[t, a] = olds[a, :, col]
        return carry

    lax.fori_loop(0, TILES, stage, 0)
    for t in range(TILES, CHIPS):
        total[t] = jnp.zeros((HALF, LANE), F32)

    pl.semaphore_wait(barrier, 1 + NX - 1 + NZ - 1 + NY - 1)

    @pl.when(c == 0)
    def _():
        for k, (first, rows) in enumerate(CHUNKS):
            rows = min(rows, 224 - first)
            send(g.at[0, SECOND + first : SECOND + first + rows], raw.at[first : first + rows], raw_s.at[k], raw_r.at[k], chip, 1).start()
        send(tail, raw.at[224:240], raw_s.at[NC - 1], raw_r.at[NC - 1], chip, 1).start()

    @pl.when(c == 1)
    def _():
        for k, (first, rows) in enumerate(CHUNKS):
            send(g.at[0, first : first + rows], raw.at[first : first + rows], raw_s.at[k], raw_r.at[k], chip, 0).start()

    @pl.when(c == 0)
    def _():
        pltpu.make_async_copy(mine_g, mine_g, own_g).wait()

    @pl.when(c == 1)
    def _():
        pltpu.make_async_copy(mine_g.at[0:224], mine_g.at[0:224], own_g).wait()

    for d in range(1, NX):
        pl.semaphore_signal(col_s, inc=1, device_id=(((x + d) % NX * NZ + z) * 2 + c, y), device_id_type=MESH)

    pl.semaphore_wait(col_s, NX - 1)

    def state_out(d, carry):
        to = (chip + d) % CHIPS

        @pl.when(to < TILES)
        def _():
            send(stg.at[to], st.at[c, chip], s1_s, s1_r, to).start()

        return carry

    lax.fori_loop(1, CHIPS, state_out, 0)

    @pl.when(chip < TILES)
    def _():
        pltpu.make_async_copy(stg.at[chip], st.at[c, chip], s1_r).start()

    right_x, left_x, far_x = (x + 1) % NX, (x + 3) % NX, (x + 2) % NX
    right_chip, left_chip = right_x * NZ + z, left_x * NZ + z

    def pair(k):
        first, rows = CHUNKS[k]
        at = slice(first, first + rows)
        arrived(raw.at[at], raw_r.at[k])

        def add(t, top):
            col = pl.ds(pl.multiple_of(t * LANE, LANE), LANE)
            value = mine_g[at, col].astype(F32) + raw[at, col].astype(F32)
            total[t, at] = value
            return jnp.maximum(top, jnp.abs(value))

        top = lax.fori_loop(0, TILES, add, jnp.zeros((rows, LANE), F32))
        top = jnp.maximum(jnp.max(top, axis=0, keepdims=True), 1e-30)
        scl[k] = top / LEVEL
        inverse = LEVEL / top

        def code(t, carry):
            acode[t, at] = encode(total[far_x * NZ + t, at], inverse)
            return carry

        lax.fori_loop(0, NZ, code, 0)
        start(acode.at[0:4, at], a_in.at[0, :, at], a_s, a_r.at[k], right_chip)
        start(acode.at[4:8, at], a_in.at[1, :, at], a_s, a_r.at[k], left_chip)
        start(scl.at[k], sa.at[0, k], as_s, as_r.at[k], right_chip)
        start(scl.at[k], sa.at[1, k], as_s, as_r.at[k], left_chip)

    def neighbours(k):
        first, rows = CHUNKS[k]
        at = slice(first, first + rows)
        arrived(a_in.at[:, :, at], a_r.at[k])
        arrived(sa.at[:, k], as_r.at[k])
        rscl[k] = scl[k] + sa[0, k]
        lscl[k] = scl[k] + sa[1, k]
        to_right, to_left = 1.0 / rscl[k], 1.0 / lscl[k]

        def code(t, carry):
            through = decode(a_in[0, t, at], sa[0, k])
            right_code[t, at] = encode(total[right_x * NZ + t, at] + through, to_right)
            right_code[t + 4, at] = encode(total[right_x * NZ + t + 4, at], to_right)
            through = decode(a_in[1, t, at], sa[1, k])
            left_code[t, at] = encode(total[left_x * NZ + t, at], to_left)
            left_code[t + 4, at] = encode(total[left_x * NZ + t + 4, at] + through, to_left)
            return carry

        lax.fori_loop(0, 4, code, 0)
        start(right_code.at[:, at], f_in.at[0, :, at], f_s, f_r.at[k], right_chip)
        start(left_code.at[:, at], f_in.at[1, :, at], f_s, f_r.at[k], left_chip)
        start(rscl.at[k], sf.at[0, k], fs_s, fs_r.at[k], right_chip)
        start(lscl.at[k], sf.at[1, k], fs_s, fs_r.at[k], left_chip)

    def along_z(k):
        first, rows = CHUNKS[k]
        at = slice(first, first + rows)
        arrived(f_in.at[:, :, at], f_r.at[k])
        arrived(sf.at[:, k], fs_r.at[k])
        zscl[k] = scl[k] + sf[0, k] + sf[1, k]
        inverse = 1.0 / zscl[k]

        def code(t, carry):
            value = total[x * NZ + t, at] + decode(f_in[0, t, at], sf[0, k]) + decode(f_in[1, t, at], sf[1, k])
            zsum[t, at] = value
            zsnd[t, at] = encode(value, inverse)
            return carry

        lax.fori_loop(0, NZ, code, 0)
        for d in range(1, NZ):
            gz = (z + d) % NZ
            to = x * NZ + gz
            start(zsnd.at[gz, at], zr.at[d - 1, at], zd_s, zd_r.at[k], to)
            start(zscl.at[k], zs.at[d - 1, k], zc_s, zc_r.at[k], to)

    pair(0)
    pair(1)
    neighbours(0)
    pair(2)
    neighbours(1)

    along_z(0)
    pair(3)
    neighbours(2)
    along_z(1)
    neighbours(3)
    along_z(2)

    @pl.when(chip < TILES)
    def _():
        arrived(st.at[c], s1_r)

    start(st.at[c], st.at[c], st_s, st_r, chip, 1 - c)
    along_z(3)
    for copy in scalars:
        copy.wait()

    arrived(st.at[1 - c], st_r)
    for a in range(3):
        new[a, 464:480] = jnp.zeros((16, LANE), F32)

    def owner_of(s, i):
        return jnp.minimum(i + (ob[i + 1] <= 4 * s).astype(I32), NODES - 1)

    def place(s, i):
        i = owner_of(s, i)
        offset = jnp.clip(4 * s - ob[i], 0, 4)
        for a in range(3):
            mat[a, pl.ds(4 * s, 4)] = st[i % 2, i // 2, a, pl.ds(offset, 4)]
        return i

    before = lax.fori_loop(0, c * (SECOND // 4), owner_of, jnp.int32(0))
    lax.fori_loop(c * (SECOND // 4), c * (SECOND // 4) + HALF // 4, place, before)

    for k, (first, rows) in enumerate(CHUNKS):
        at = slice(first, first + rows)
        arrived(zr.at[:, at], zd_r.at[k])
        arrived(zs.at[:, k], zc_r.at[k])
        value = zsum[z, at]
        for d in range(NZ - 1):
            value = value + decode(zr[d, at], zs[d, k])
        grad[at] = value

    steps = step_count[0]
    rate = learning_rate[0]
    first_left = 1.0 - power(beta_first, steps)
    second_left = 1.0 - power(beta_second, steps)

    def step(b, carry):
        rows = pl.ds(pl.multiple_of(c * SECOND + b * 48, 16), 48)
        gradient = grad[pl.ds(pl.multiple_of(b * 48, 16), 48)]
        master = mat[0, rows]
        first_new = beta_first * mat[1, rows] + (1.0 - beta_first) * gradient
        second_new = beta_second * mat[2, rows] + (1.0 - beta_second) * gradient * gradient
        first_hat = first_new / first_left
        second_hat = second_new / second_left
        new[0, rows] = master - rate * (first_hat / (jnp.sqrt(second_hat) + adam_eps) + decay * master)
        new[1, rows] = first_new
        new[2, rows] = second_new
        return carry

    lax.fori_loop(0, HALF // 48, step, 0)

    for i in range(2):
        rows = new[0, pl.ds(c * 230 + 115 * i, 120)]
        wb[i] = jnp.concatenate([rows, jnp.zeros((8, LANE), F32)], axis=0).astype(BF16)
    for dz in (0, 1, 7, 2, 6, 3, 5, 4):
        for i in range(2):
            yy = 2 * c + i
            to = x * NZ + (z + dz) % NZ
            for other in range(2):
                core = (c + other) % 2
                src = wb.at[i, pl.ds(pl.multiple_of(core * PART, PART), PART)]
                dst = blocks.at[core, x, z, y]
                if dz == 0 and other == 0:
                    @pl.when(yy == y)
                    def _():
                        pltpu.make_async_copy(src, dst, w_r.at[0]).start()

                    @pl.when(yy != y)
                    def _():
                        start(src, dst, w_s, w_r.at[0], to, core, yy)
                else:
                    start(src, dst, w_s, w_r.at[dz], to, core, yy)

    @pl.when(c == 0)
    def _():
        send(new.at[:, 0:224], peer, ex_s, ex_r, chip, 1).start()

    @pl.when(c == 1)
    def _():
        send(new.at[:, 240:464], peer, ex_s, ex_r, chip, 0).start()

    arrived(peer, ex_r)
    theirs = pl.ds(pl.multiple_of((1 - c) * HALF, 16), 224)
    for a in range(3):
        new[a, theirs] = peer[a]

    def pick(m, carry):
        begin = jnp.clip(nb[2 * m + c], 0, UNITS)
        count = nb[2 * m + c + 1] - begin
        slot = lax.broadcasted_iota(I32, (CAP_NEW, LANE), 0)
        for a in range(3):
            rows = new[a, pl.ds(begin, CAP_NEW)]
            snd[m, CAP_NEW * a : CAP_NEW * (a + 1)] = jnp.where(slot < count, rows, 0.0)
        return carry

    lax.fori_loop(0, OWNERS // 2, pick, 0)

    def share(ref):
        start(ref, ref, cx_s, cx_r, chip, 1 - c)

    def spread(at, e):
        ref = blocks.at[c, x, at]
        start(ref, ref, x_s, x_r.at[0, e], right_chip)
        start(ref, ref, x_s, x_r.at[1, e], left_chip)
        share(ref)

    def relay(at, e):
        arrived(blocks.at[c, left_x, at], x_r.at[0, e])
        half = blocks.at[c, left_x, at, 0:2]
        start(half, half, far_s, far_r.at[e], right_chip)
        arrived(blocks.at[c, right_x, at], x_r.at[1, e])
        half = blocks.at[c, right_x, at, 2:4]
        start(half, half, far_s, far_r.at[e], left_chip)
        share(blocks.at[c, left_x, at])
        share(blocks.at[c, right_x, at])

    owner = (48 - c - chip) % CHIPS

    def owners_out(d, carry):
        to = (chip + d) % CHIPS
        m = (48 - c - to) % CHIPS

        @pl.when((m < OWNERS // 2) & (chip < TILES))
        def _():
            send(snd.at[m], r2.at[chip], s2_s, s2_r, to).start()

        return carry

    @pl.when((owner < OWNERS // 2) & (chip < TILES))
    def _():
        pltpu.make_async_copy(snd.at[owner], r2.at[chip], s2_r).start()

    lax.fori_loop(1, CHIPS, owners_out, 0)

    order = (0, 1, 7, 2, 6, 3, 5, 4)
    for n, dz in enumerate(order):
        at = (z + NZ - dz) % NZ
        arrived(blocks.at[c, x, at], w_r.at[dz])
        spread(at, dz)
        if n >= 2:
            relay((z + NZ - order[n - 2]) % NZ, order[n - 2])

    for dz in order[6:]:
        relay((z + NZ - dz) % NZ, dz)

    for dz in order:
        ref = blocks.at[c, far_x, (z + NZ - dz) % NZ]
        arrived(ref, far_r.at[dz])
        share(ref)

    @pl.when(owner < OWNERS // 2)
    def _():
        arrived(r2.at[0:TILES], s2_r)

    @pl.when(owner >= OWNERS // 2)
    def _():
        zero[...] = jnp.zeros_like(zero)
        clear = pltpu.make_async_copy(zero, r2.at[0:TILES], s2_r)
        clear.start()
        clear.wait()

    @pl.when((owner < OWNERS // 2) & (chip < TILES))
    def _():
        arrived(snd.at[0:25], s2_s)

    @pl.when((owner >= OWNERS // 2) & (chip < TILES))
    def _():
        arrived(snd.at[0:26], s2_s)

    arrived(blocks.at[1 - c], cx_r)
    for k, (first, rows) in enumerate(CHUNKS):
        arrived(raw.at[first : first + rows], raw_s.at[k])

    @pl.when(chip < TILES)
    def _():
        arrived(stg.at[0:28], s1_s)

    @pl.when(chip >= TILES)
    def _():
        arrived(stg.at[0:29], s1_s)

    @pl.when(y // 2 != c)
    def _():
        arrived(blocks.at[c, 0], w_s)

    @pl.when(y // 2 == c)
    def _():
        arrived(total.at[0:31, 0:32], w_s)

    for ref, sem in (
        (acode, a_s), (sa, as_s), (f_in, f_s), (sf, fs_s), (zr, zd_s), (zs, zc_s), (st.at[c], st_s),
        (peer, ex_s), (blocks.at[c, 0:2], x_s), (blocks.at[c, 0], far_s), (blocks.at[c], cx_s),
    ):
        arrived(ref, sem)


def lay_out(blocks, r2, o_m, o_f, o_s, o_w, got, rows, state, wide, in_s, out_s):
    copies = [pltpu.make_async_copy(blocks.at[:, :, :, q], got.at[q], in_s.at[q]) for q in range(NY)]
    copies.append(pltpu.make_async_copy(r2, rows, in_s.at[NY]))
    for copy in copies:
        copy.start()
    outs = []

    def out(src, dst):
        outs.append(pltpu.make_async_copy(src, dst, out_s.at[len(outs)]))
        outs[-1].start()

    for q in range(NY):
        copies[q].wait()
        for t in range(TILES):
            col = slice(t * LANE, (t + 1) * LANE)
            wide[q, 0:64, col] = got[q, 0, t // NZ, t % NZ]
            wide[q, 64:115, col] = got[q, 1, t // NZ, t % NZ, 0:51]
        out(wide.at[q], o_w.at[:, q * WIDTH : (q + 1) * WIDTH])

    copies[NY].wait()

    def tile(t, carry):
        for a in range(3):
            for s in range(CAP_NEW):
                state[a, s, t] = rows[t, CAP_NEW * a + s : CAP_NEW * a + s + 1]
        return carry

    lax.fori_loop(0, TILES, tile, 0)
    for a, dst in enumerate((o_m, o_f, o_s)):
        out(state.at[a], dst)
    for copy in outs:
        copy.wait()


def on_device(grad_partials, old_master, old_first, old_second, old_bounds, new_bounds, step_count, learning_rate):
    dma = pltpu.SemaphoreType.DMA
    hbm = pl.BlockSpec(memory_space=pl.ANY)
    scale = pltpu.VMEM((NC, 1, LANE), F32)
    scratch = [
        pltpu.SMEM((NODES + 1,), I32),
        pltpu.SMEM((OWNERS + 1,), I32),
        pltpu.SMEM((1,), I32),
        pltpu.SMEM((1,), F32),
        pltpu.VMEM((HALF, WIDTH), BF16),
        pltpu.VMEM((HALF, WIDTH), BF16),
        pltpu.VMEM((16, WIDTH), BF16),
        pltpu.VMEM((3, 8, WIDTH), F32),
        pltpu.VMEM((CHIPS, HALF, LANE), F32),
        pltpu.VMEM((NZ, HALF, LANE), I16),
        pltpu.VMEM((NZ, HALF, LANE), I16),
        pltpu.VMEM((NZ, HALF, LANE), I16),
        scale, scale, scale,
        pltpu.VMEM((2, NZ // 2, HALF, LANE), I16),
        pltpu.VMEM((2, NC, 1, LANE), F32),
        pltpu.VMEM((2, NZ, HALF, LANE), I16),
        pltpu.VMEM((2, NC, 1, LANE), F32),
        pltpu.VMEM((NZ, HALF, LANE), F32),
        pltpu.VMEM((NZ, HALF, LANE), I16),
        scale,
        pltpu.VMEM((NZ - 1, HALF, LANE), I16),
        pltpu.VMEM((NZ - 1, NC, 1, LANE), F32),
        pltpu.VMEM((HALF, LANE), F32),
        pltpu.VMEM((CHIPS, 3, 8, LANE), F32),
        pltpu.VMEM((2, CHIPS, 3, 8, LANE), F32),
        pltpu.VMEM((3, 480, LANE), F32),
        pltpu.VMEM((3, 480, LANE), F32),
        pltpu.VMEM((3, 224, LANE), F32),
        pltpu.VMEM((2, 128, LANE), BF16),
        pltpu.VMEM((OWNERS // 2, 3 * CAP_NEW, LANE), F32),
        pltpu.VMEM((TILES, 3 * CAP_NEW, LANE), F32),
        dma((4,)), pltpu.SemaphoreType.REGULAR,
        dma((3,)), dma,
        dma((NC,)), dma((NC,)),
        dma, dma((NC,)), dma, dma((NC,)), dma, dma((NC,)), dma, dma((NC,)),
        dma, dma((NC,)), dma, dma((NC,)),
        dma, dma, dma, dma, dma, dma,
        dma, dma((NZ,)), dma, dma((2, NZ)), dma, dma((NZ,)), dma, dma,
        dma, dma,
    ]
    blocks, r2 = pl.pallas_call(
        kernel,
        name="adamw_move",
        out_shape=(
            jax.ShapeDtypeStruct((2, NX, NZ, NY, PART, LANE), BF16),
            jax.ShapeDtypeStruct((CHIPS, 3 * CAP_NEW, LANE), F32),
        ),
        in_specs=[hbm, hbm, hbm, hbm, hbm, pl.BlockSpec((1, 16, WIDTH), lambda i: (0, 28, 0)), hbm, hbm, hbm],
        grid=(1,),
        out_specs=(hbm, hbm),
        scratch_shapes=scratch,
        compiler_params=pltpu.CompilerParams(collective_id=0, has_side_effects=True, vmem_limit_bytes=56 * 2**20),
    )(old_bounds, new_bounds, step_count, learning_rate, grad_partials, grad_partials, old_master, old_first, old_second)
    rows = jax.ShapeDtypeStruct((CAP_NEW, TILES, 1, LANE), F32)
    outs = pl.pallas_call(
        lay_out,
        name="lay_out",
        out_shape=(rows, rows, rows, jax.ShapeDtypeStruct((115, NY * WIDTH), BF16)),
        in_specs=[hbm, hbm],
        out_specs=(hbm, hbm, hbm, hbm),
        scratch_shapes=[
            pltpu.VMEM((NY, 2, NX, NZ, PART, LANE), BF16),
            pltpu.VMEM((CHIPS, 3 * CAP_NEW, LANE), F32),
            pltpu.VMEM((3, CAP_NEW, TILES, 1, LANE), F32),
            pltpu.VMEM((NY, 115, WIDTH), BF16),
            dma((NY + 1,)),
            dma((NY + 3,)),
        ],
        compiler_params=pltpu.CompilerParams(vmem_limit_bytes=60 * 2**20),
    )(blocks, r2)
    return tuple(out.reshape(1, CAP_NEW, WIDTH) for out in outs[:3]) + (outs[3],)


def solution(mesh):
    split = P("node", None, "local")
    return jax.shard_map(
        on_device,
        mesh=mesh,
        in_specs=(split, split, split, split, P(), P(), P(), P()),
        out_specs=(split, split, split, P("local", None)),
        check_vma=False,
    )
```

```python
import jax
import jax.numpy as jnp
from jax import lax
from jax.experimental import pallas as pl
from jax.experimental.pallas import tpu as pltpu
from jax.sharding import PartitionSpec as P

MESH = pl.DeviceIdType.MESH
F32, BF16, I16, I32 = jnp.float32, jnp.bfloat16, jnp.int16, jnp.int32

UNITS = 460
WIDTH = 3712
LANE = 128
TILES = WIDTH // LANE
NODES = 64
CHIPS = 32
NX, NZ, NY = 4, 8, 4
HALF = 240
SECOND = 224
CHUNKS = ((0, 64), (64, 64), (128, 64), (192, 48))
NC = len(CHUNKS)
SEGMENTS = 115
CAP_NEW = 12
OWNERS = 52
PART = 64
LEVEL = 32760.0

beta_first = 0.9
beta_second = 0.95
adam_eps = 1e-08
decay = 0.1


def power(base, steps):
    result = jnp.float32(1.0)
    factor = float(base)
    for bit in range(5):
        result = jnp.where((steps // (1 << bit)) % 2 == 1, result * jnp.float32(factor), result)
        factor = factor * factor
    return result


def encode(value, inverse):
    return jnp.round(value * inverse).astype(I32).astype(I16)


def decode(code, scale):
    return code.astype(I32).astype(F32) * scale


def kernel(
    ob_in, nb_in, steps_in, rate_in, g, end, om, of, os_,
    blocks, r2,
    ob, nb, step_count, learning_rate,
    mine_g, raw, tail, olds, total, acode, right_code, left_code, scl, rscl, lscl, a_in, sa, f_in, sf,
    zsum, zsnd, zscl, zr, zs, grad,
    stg, st, mat, new, peer, wb, snd, zero,
    sc_s, col_s, in_s, own_g, raw_s, raw_r, a_s, a_r, as_s, as_r, f_s, f_r, fs_s, fs_r, zd_s, zd_r, zc_s, zc_r,
    s1_s, s1_r, st_s, st_r, ex_s, ex_r, w_s, w_r, x_s, x_r, far_s, far_r, cx_s, cx_r, s2_s, s2_r,
):
    node, y = lax.axis_index("node"), lax.axis_index("local")
    c, chip = node % 2, node // 2
    x, z = chip // NZ, chip % NZ

    def send(src, dst, ss, rs, to_chip, to_core=None, to_y=None):
        core = c if to_core is None else to_core
        return pltpu.make_async_remote_copy(
            src_ref=src, dst_ref=dst, send_sem=ss, recv_sem=rs,
            device_id=(to_chip * 2 + core, y if to_y is None else to_y), device_id_type=MESH,
        )

    def start(src, dst, ss, rs, to_chip, to_core=None, to_y=None):
        send(src, dst, ss, rs, to_chip, to_core, to_y).start()

    def arrived(ref, sem):
        pltpu.make_async_copy(ref, ref, sem).wait()

    barrier = pltpu.get_barrier_semaphore()

    def greet(to_chip, to_core, to_y):
        pl.semaphore_signal(barrier, inc=1, device_id=(to_chip * 2 + to_core, to_y), device_id_type=MESH)

    greet(chip, 1 - c, y)
    for d in range(1, NX):
        greet((x + d) % NX * NZ + z, c, y)
    for d in range(1, NZ):
        greet(x * NZ + (z + d) % NZ, c, y)
    for d in range(1, NY):
        greet(chip, c, (y + d) % NY)

    scalars = [
        pltpu.make_async_copy(src, dst, sc_s.at[a])
        for a, (src, dst) in enumerate(((ob_in, ob), (nb_in, nb), (steps_in, step_count), (rate_in, learning_rate)))
    ]
    for copy in scalars:
        copy.start()
    state_in = [pltpu.make_async_copy(old.at[0], olds.at[a], in_s.at[a]) for a, old in enumerate((om, of, os_))]
    for copy in state_in:
        copy.start()
    row = lax.broadcasted_iota(I32, (16, WIDTH), 0)
    tail[...] = jnp.where(row < 12, end[0].astype(F32), 0.0).astype(BF16)

    @pl.when(c == 0)
    def _():
        pltpu.make_async_copy(g.at[0, 0:HALF], mine_g, own_g).start()

    @pl.when(c == 1)
    def _():
        pltpu.make_async_copy(g.at[0, SECOND:448], mine_g.at[0:224], own_g).start()
        mine_g[224:240] = tail[...]

    for copy in state_in:
        copy.wait()

    def stage(t, carry):
        col = pl.ds(pl.multiple_of(t * LANE, LANE), LANE)
        for a in range(3):
            stg[t, a] = olds[a, :, col]
        return carry

    lax.fori_loop(0, TILES, stage, 0)
    for t in range(TILES, CHIPS):
        total[t] = jnp.zeros((HALF, LANE), F32)

    pl.semaphore_wait(barrier, 1 + NX - 1 + NZ - 1 + NY - 1)

    @pl.when(c == 0)
    def _():
        for k, (first, rows) in enumerate(CHUNKS):
            rows = min(rows, 224 - first)
            send(g.at[0, SECOND + first : SECOND + first + rows], raw.at[first : first + rows], raw_s.at[k], raw_r.at[k], chip, 1).start()
        send(tail, raw.at[224:240], raw_s.at[NC - 1], raw_r.at[NC - 1], chip, 1).start()

    @pl.when(c == 1)
    def _():
        for k, (first, rows) in enumerate(CHUNKS):
            send(g.at[0, first : first + rows], raw.at[first : first + rows], raw_s.at[k], raw_r.at[k], chip, 0).start()

    @pl.when(c == 0)
    def _():
        pltpu.make_async_copy(mine_g, mine_g, own_g).wait()

    @pl.when(c == 1)
    def _():
        pltpu.make_async_copy(mine_g.at[0:224], mine_g.at[0:224], own_g).wait()

    for d in range(1, NX):
        pl.semaphore_signal(col_s, inc=1, device_id=(((x + d) % NX * NZ + z) * 2 + c, y), device_id_type=MESH)

    pl.semaphore_wait(col_s, NX - 1)

    def state_out(d, carry):
        to = (chip + d) % CHIPS

        @pl.when(to < TILES)
        def _():
            send(stg.at[to], st.at[c, chip], s1_s, s1_r, to).start()

        return carry

    lax.fori_loop(1, CHIPS, state_out, 0)

    @pl.when(chip < TILES)
    def _():
        pltpu.make_async_copy(stg.at[chip], st.at[c, chip], s1_r).start()

    right_x, left_x, far_x = (x + 1) % NX, (x + 3) % NX, (x + 2) % NX
    right_chip, left_chip = right_x * NZ + z, left_x * NZ + z

    def pair(k):
        first, rows = CHUNKS[k]
        at = slice(first, first + rows)
        arrived(raw.at[at], raw_r.at[k])

        def add(t, top):
            col = pl.ds(pl.multiple_of(t * LANE, LANE), LANE)
            value = mine_g[at, col].astype(F32) + raw[at, col].astype(F32)
            total[t, at] = value
            return jnp.maximum(top, jnp.abs(value))

        top = lax.fori_loop(0, TILES, add, jnp.zeros((rows, LANE), F32))
        top = jnp.maximum(jnp.max(top, axis=0, keepdims=True), 1e-30)
        scl[k] = top / LEVEL
        inverse = LEVEL / top

        def code(t, carry):
            acode[t, at] = encode(total[far_x * NZ + t, at], inverse)
            return carry

        lax.fori_loop(0, NZ, code, 0)
        start(acode.at[0:4, at], a_in.at[0, :, at], a_s, a_r.at[k], right_chip)
        start(acode.at[4:8, at], a_in.at[1, :, at], a_s, a_r.at[k], left_chip)
        start(scl.at[k], sa.at[0, k], as_s, as_r.at[k], right_chip)
        start(scl.at[k], sa.at[1, k], as_s, as_r.at[k], left_chip)

    def neighbours(k):
        first, rows = CHUNKS[k]
        at = slice(first, first + rows)
        arrived(a_in.at[:, :, at], a_r.at[k])
        arrived(sa.at[:, k], as_r.at[k])
        rscl[k] = scl[k] + sa[0, k]
        lscl[k] = scl[k] + sa[1, k]
        to_right, to_left = 1.0 / rscl[k], 1.0 / lscl[k]

        def code(t, carry):
            through = decode(a_in[0, t, at], sa[0, k])
            right_code[t, at] = encode(total[right_x * NZ + t, at] + through, to_right)
            right_code[t + 4, at] = encode(total[right_x * NZ + t + 4, at], to_right)
            through = decode(a_in[1, t, at], sa[1, k])
            left_code[t, at] = encode(total[left_x * NZ + t, at], to_left)
            left_code[t + 4, at] = encode(total[left_x * NZ + t + 4, at] + through, to_left)
            return carry

        lax.fori_loop(0, 4, code, 0)
        start(right_code.at[:, at], f_in.at[0, :, at], f_s, f_r.at[k], right_chip)
        start(left_code.at[:, at], f_in.at[1, :, at], f_s, f_r.at[k], left_chip)
        start(rscl.at[k], sf.at[0, k], fs_s, fs_r.at[k], right_chip)
        start(lscl.at[k], sf.at[1, k], fs_s, fs_r.at[k], left_chip)

    def along_z(k):
        first, rows = CHUNKS[k]
        at = slice(first, first + rows)
        arrived(f_in.at[:, :, at], f_r.at[k])
        arrived(sf.at[:, k], fs_r.at[k])
        zscl[k] = scl[k] + sf[0, k] + sf[1, k]
        inverse = 1.0 / zscl[k]

        def code(t, carry):
            value = total[x * NZ + t, at] + decode(f_in[0, t, at], sf[0, k]) + decode(f_in[1, t, at], sf[1, k])
            zsum[t, at] = value
            zsnd[t, at] = encode(value, inverse)
            return carry

        lax.fori_loop(0, NZ, code, 0)
        for d in range(1, NZ):
            gz = (z + d) % NZ
            to = x * NZ + gz
            start(zsnd.at[gz, at], zr.at[d - 1, at], zd_s, zd_r.at[k], to)
            start(zscl.at[k], zs.at[d - 1, k], zc_s, zc_r.at[k], to)

    pair(0)
    pair(1)
    neighbours(0)
    pair(2)
    neighbours(1)

    along_z(0)
    pair(3)
    neighbours(2)
    along_z(1)
    neighbours(3)
    along_z(2)

    @pl.when(chip < TILES)
    def _():
        arrived(st.at[c], s1_r)

    start(st.at[c], st.at[c], st_s, st_r, chip, 1 - c)
    along_z(3)
    for copy in scalars:
        copy.wait()

    arrived(st.at[1 - c], st_r)
    for a in range(3):
        new[a, 464:480] = jnp.zeros((16, LANE), F32)

    def owner_of(s, i):
        return jnp.minimum(i + (ob[i + 1] <= 4 * s).astype(I32), NODES - 1)

    def place(s, i):
        i = owner_of(s, i)
        offset = jnp.clip(4 * s - ob[i], 0, 4)
        for a in range(3):
            mat[a, pl.ds(4 * s, 4)] = st[i % 2, i // 2, a, pl.ds(offset, 4)]
        return i

    before = lax.fori_loop(0, c * (SECOND // 4), owner_of, jnp.int32(0))
    lax.fori_loop(c * (SECOND // 4), c * (SECOND // 4) + HALF // 4, place, before)

    for k, (first, rows) in enumerate(CHUNKS):
        at = slice(first, first + rows)
        arrived(zr.at[:, at], zd_r.at[k])
        arrived(zs.at[:, k], zc_r.at[k])
        value = zsum[z, at]
        for d in range(NZ - 1):
            value = value + decode(zr[d, at], zs[d, k])
        grad[at] = value

    steps = step_count[0]
    rate = learning_rate[0]
    first_left = 1.0 - power(beta_first, steps)
    second_left = 1.0 - power(beta_second, steps)

    def step(b, carry):
        rows = pl.ds(pl.multiple_of(c * SECOND + b * 48, 16), 48)
        gradient = grad[pl.ds(pl.multiple_of(b * 48, 16), 48)]
        master = mat[0, rows]
        first_new = beta_first * mat[1, rows] + (1.0 - beta_first) * gradient
        second_new = beta_second * mat[2, rows] + (1.0 - beta_second) * gradient * gradient
        first_hat = first_new / first_left
        second_hat = second_new / second_left
        new[0, rows] = master - rate * (first_hat / (jnp.sqrt(second_hat) + adam_eps) + decay * master)
        new[1, rows] = first_new
        new[2, rows] = second_new
        return carry

    lax.fori_loop(0, HALF // 48, step, 0)

    for i in range(2):
        rows = new[0, pl.ds(c * 230 + 115 * i, 120)]
        wb[i] = jnp.concatenate([rows, jnp.zeros((8, LANE), F32)], axis=0).astype(BF16)
    for dz in (0, 1, 7, 2, 6, 3, 5, 4):
        for i in range(2):
            yy = 2 * c + i
            to = x * NZ + (z + dz) % NZ
            for other in range(2):
                core = (c + other) % 2
                src = wb.at[i, pl.ds(pl.multiple_of(core * PART, PART), PART)]
                dst = blocks.at[core, x, z, y]
                if dz == 0 and other == 0:
                    @pl.when(yy == y)
                    def _():
                        pltpu.make_async_copy(src, dst, w_r.at[0]).start()

                    @pl.when(yy != y)
                    def _():
                        start(src, dst, w_s, w_r.at[0], to, core, yy)
                else:
                    start(src, dst, w_s, w_r.at[dz], to, core, yy)

    @pl.when(c == 0)
    def _():
        send(new.at[:, 0:224], peer, ex_s, ex_r, chip, 1).start()

    @pl.when(c == 1)
    def _():
        send(new.at[:, 240:464], peer, ex_s, ex_r, chip, 0).start()

    arrived(peer, ex_r)
    theirs = pl.ds(pl.multiple_of((1 - c) * HALF, 16), 224)
    for a in range(3):
        new[a, theirs] = peer[a]

    def pick(m, carry):
        begin = jnp.clip(nb[2 * m + c], 0, UNITS)
        count = nb[2 * m + c + 1] - begin
        slot = lax.broadcasted_iota(I32, (CAP_NEW, LANE), 0)
        for a in range(3):
            rows = new[a, pl.ds(begin, CAP_NEW)]
            snd[m, CAP_NEW * a : CAP_NEW * (a + 1)] = jnp.where(slot < count, rows, 0.0)
        return carry

    lax.fori_loop(0, OWNERS // 2, pick, 0)

    def share(ref):
        start(ref, ref, cx_s, cx_r, chip, 1 - c)

    def spread(at, e):
        ref = blocks.at[c, x, at]
        start(ref, ref, x_s, x_r.at[0, e], right_chip)
        start(ref, ref, x_s, x_r.at[1, e], left_chip)
        share(ref)

    def relay(at, e):
        arrived(blocks.at[c, left_x, at], x_r.at[0, e])
        half = blocks.at[c, left_x, at, 0:2]
        start(half, half, far_s, far_r.at[e], right_chip)
        arrived(blocks.at[c, right_x, at], x_r.at[1, e])
        half = blocks.at[c, right_x, at, 2:4]
        start(half, half, far_s, far_r.at[e], left_chip)
        share(blocks.at[c, left_x, at])
        share(blocks.at[c, right_x, at])

    owner = (48 - c - chip) % CHIPS

    def owners_out(d, carry):
        to = (chip + d) % CHIPS
        m = (48 - c - to) % CHIPS

        @pl.when((m < OWNERS // 2) & (chip < TILES))
        def _():
            send(snd.at[m], r2.at[chip], s2_s, s2_r, to).start()

        return carry

    @pl.when((owner < OWNERS // 2) & (chip < TILES))
    def _():
        pltpu.make_async_copy(snd.at[owner], r2.at[chip], s2_r).start()

    lax.fori_loop(1, CHIPS, owners_out, 0)

    order = (0, 1, 7, 2, 6, 3, 5, 4)
    for n, dz in enumerate(order):
        at = (z + NZ - dz) % NZ
        arrived(blocks.at[c, x, at], w_r.at[dz])
        spread(at, dz)
        if n >= 2:
            relay((z + NZ - order[n - 2]) % NZ, order[n - 2])

    for dz in order[6:]:
        relay((z + NZ - dz) % NZ, dz)

    for dz in order:
        ref = blocks.at[c, far_x, (z + NZ - dz) % NZ]
        arrived(ref, far_r.at[dz])
        share(ref)

    @pl.when(owner < OWNERS // 2)
    def _():
        arrived(r2.at[0:TILES], s2_r)

    @pl.when(owner >= OWNERS // 2)
    def _():
        zero[...] = jnp.zeros_like(zero)
        clear = pltpu.make_async_copy(zero, r2.at[0:TILES], s2_r)
        clear.start()
        clear.wait()

    @pl.when((owner < OWNERS // 2) & (chip < TILES))
    def _():
        arrived(snd.at[0:25], s2_s)

    @pl.when((owner >= OWNERS // 2) & (chip < TILES))
    def _():
        arrived(snd.at[0:26], s2_s)

    arrived(blocks.at[1 - c], cx_r)
    for k, (first, rows) in enumerate(CHUNKS):
        arrived(raw.at[first : first + rows], raw_s.at[k])

    @pl.when(chip < TILES)
    def _():
        arrived(stg.at[0:28], s1_s)

    @pl.when(chip >= TILES)
    def _():
        arrived(stg.at[0:29], s1_s)

    @pl.when(y // 2 != c)
    def _():
        arrived(blocks.at[c, 0], w_s)

    @pl.when(y // 2 == c)
    def _():
        arrived(total.at[0:31, 0:32], w_s)

    for ref, sem in (
        (acode, a_s), (sa, as_s), (f_in, f_s), (sf, fs_s), (zr, zd_s), (zs, zc_s), (st.at[c], st_s),
        (peer, ex_s), (blocks.at[c, 0:2], x_s), (blocks.at[c, 0], far_s), (blocks.at[c], cx_s),
    ):
        arrived(ref, sem)


def lay_out(blocks, r2, o_m, o_f, o_s, o_w, got, rows, state, wide, in_s, out_s):
    here = pltpu.make_async_copy(r2, rows, in_s.at[NY])
    here.start()
    copies = [pltpu.make_async_copy(blocks.at[:, :, :, q], got.at[q], in_s.at[q]) for q in range(NY)]
    for copy in copies:
        copy.start()
    outs = []

    def out(src, dst):
        outs.append(pltpu.make_async_copy(src, dst, out_s.at[len(outs)]))
        outs[-1].start()

    here.wait()

    def tile(t, carry):
        for a in range(3):
            for s in range(CAP_NEW):
                state[a, s, t] = rows[t, CAP_NEW * a + s : CAP_NEW * a + s + 1]
        return carry

    lax.fori_loop(0, TILES, tile, 0)
    for a, dst in enumerate((o_m, o_f, o_s)):
        out(state.at[a], dst)
    for q in range(NY):
        copies[q].wait()
        for t in range(TILES):
            col = slice(t * LANE, (t + 1) * LANE)
            wide[q, 0:64, col] = got[q, 0, t // NZ, t % NZ]
            wide[q, 64:115, col] = got[q, 1, t // NZ, t % NZ, 0:51]
        out(wide.at[q], o_w.at[:, q * WIDTH : (q + 1) * WIDTH])
    for copy in outs:
        copy.wait()


def on_device(grad_partials, old_master, old_first, old_second, old_bounds, new_bounds, step_count, learning_rate):
    dma = pltpu.SemaphoreType.DMA
    hbm = pl.BlockSpec(memory_space=pl.ANY)
    scale = pltpu.VMEM((NC, 1, LANE), F32)
    scratch = [
        pltpu.SMEM((NODES + 1,), I32),
        pltpu.SMEM((OWNERS + 1,), I32),
        pltpu.SMEM((1,), I32),
        pltpu.SMEM((1,), F32),
        pltpu.VMEM((HALF, WIDTH), BF16),
        pltpu.VMEM((HALF, WIDTH), BF16),
        pltpu.VMEM((16, WIDTH), BF16),
        pltpu.VMEM((3, 8, WIDTH), F32),
        pltpu.VMEM((CHIPS, HALF, LANE), F32),
        pltpu.VMEM((NZ, HALF, LANE), I16),
        pltpu.VMEM((NZ, HALF, LANE), I16),
        pltpu.VMEM((NZ, HALF, LANE), I16),
        scale, scale, scale,
        pltpu.VMEM((2, NZ // 2, HALF, LANE), I16),
        pltpu.VMEM((2, NC, 1, LANE), F32),
        pltpu.VMEM((2, NZ, HALF, LANE), I16),
        pltpu.VMEM((2, NC, 1, LANE), F32),
        pltpu.VMEM((NZ, HALF, LANE), F32),
        pltpu.VMEM((NZ, HALF, LANE), I16),
        scale,
        pltpu.VMEM((NZ - 1, HALF, LANE), I16),
        pltpu.VMEM((NZ - 1, NC, 1, LANE), F32),
        pltpu.VMEM((HALF, LANE), F32),
        pltpu.VMEM((CHIPS, 3, 8, LANE), F32),
        pltpu.VMEM((2, CHIPS, 3, 8, LANE), F32),
        pltpu.VMEM((3, 480, LANE), F32),
        pltpu.VMEM((3, 480, LANE), F32),
        pltpu.VMEM((3, 224, LANE), F32),
        pltpu.VMEM((2, 128, LANE), BF16),
        pltpu.VMEM((OWNERS // 2, 3 * CAP_NEW, LANE), F32),
        pltpu.VMEM((TILES, 3 * CAP_NEW, LANE), F32),
        dma((4,)), pltpu.SemaphoreType.REGULAR,
        dma((3,)), dma,
        dma((NC,)), dma((NC,)),
        dma, dma((NC,)), dma, dma((NC,)), dma, dma((NC,)), dma, dma((NC,)),
        dma, dma((NC,)), dma, dma((NC,)),
        dma, dma, dma, dma, dma, dma,
        dma, dma((NZ,)), dma, dma((2, NZ)), dma, dma((NZ,)), dma, dma,
        dma, dma,
    ]
    blocks, r2 = pl.pallas_call(
        kernel,
        name="adamw_move",
        out_shape=(
            jax.ShapeDtypeStruct((2, NX, NZ, NY, PART, LANE), BF16),
            jax.ShapeDtypeStruct((CHIPS, 3 * CAP_NEW, LANE), F32),
        ),
        in_specs=[hbm, hbm, hbm, hbm, hbm, pl.BlockSpec((1, 16, WIDTH), lambda i: (0, 28, 0)), hbm, hbm, hbm],
        grid=(1,),
        out_specs=(hbm, hbm),
        scratch_shapes=scratch,
        compiler_params=pltpu.CompilerParams(collective_id=0, has_side_effects=True, vmem_limit_bytes=56 * 2**20),
    )(old_bounds, new_bounds, step_count, learning_rate, grad_partials, grad_partials, old_master, old_first, old_second)
    rows = jax.ShapeDtypeStruct((CAP_NEW, TILES, 1, LANE), F32)
    outs = pl.pallas_call(
        lay_out,
        name="lay_out",
        out_shape=(rows, rows, rows, jax.ShapeDtypeStruct((115, NY * WIDTH), BF16)),
        in_specs=[hbm, hbm],
        out_specs=(hbm, hbm, hbm, hbm),
        scratch_shapes=[
            pltpu.VMEM((NY, 2, NX, NZ, PART, LANE), BF16),
            pltpu.VMEM((CHIPS, 3 * CAP_NEW, LANE), F32),
            pltpu.VMEM((3, CAP_NEW, TILES, 1, LANE), F32),
            pltpu.VMEM((NY, 115, WIDTH), BF16),
            dma((NY + 1,)),
            dma((NY + 3,)),
        ],
        compiler_params=pltpu.CompilerParams(vmem_limit_bytes=60 * 2**20),
    )(blocks, r2)
    return tuple(out.reshape(1, CAP_NEW, WIDTH) for out in outs[:3]) + (outs[3],)


def solution(mesh):
    split = P("node", None, "local")
    return jax.shard_map(
        on_device,
        mesh=mesh,
        in_specs=(split, split, split, split, P(), P(), P(), P()),
        out_specs=(split, split, split, P("local", None)),
        check_vma=False,
    )
```

```python
import jax
import jax.numpy as jnp
from jax import lax
from jax.experimental import pallas as pl
from jax.experimental.pallas import tpu as pltpu
from jax.sharding import PartitionSpec as P

MESH = pl.DeviceIdType.MESH
F32, BF16, I16, I32 = jnp.float32, jnp.bfloat16, jnp.int16, jnp.int32

UNITS = 460
WIDTH = 3712
LANE = 128
TILES = WIDTH // LANE
NODES = 64
CHIPS = 32
NX, NZ, NY = 4, 8, 4
HALF = 240
SECOND = 224
CHUNKS = ((0, 64), (64, 64), (128, 64), (192, 48))
NC = len(CHUNKS)
SEGMENTS = 115
CAP_NEW = 12
OWNERS = 52
PART = 64
LEVEL = 32760.0

beta_first = 0.9
beta_second = 0.95
adam_eps = 1e-08
decay = 0.1


def power(base, steps):
    result = jnp.float32(1.0)
    factor = float(base)
    for bit in range(5):
        result = jnp.where((steps // (1 << bit)) % 2 == 1, result * jnp.float32(factor), result)
        factor = factor * factor
    return result


def encode(value, inverse):
    return jnp.round(value * inverse).astype(I32).astype(I16)


def decode(code, scale):
    return code.astype(I32).astype(F32) * scale


def kernel(
    ob_in, nb_in, steps_in, rate_in, g, end, om, of, os_,
    blocks, r2,
    ob, nb, step_count, learning_rate,
    mine_g, raw, tail, olds, total, acode, right_code, left_code, scl, rscl, lscl, a_in, sa, f_in, sf,
    zsum, zsnd, zscl, zr, zs, grad,
    stg, st, mat, new, peer, wb, snd, zero,
    sc_s, col_s, in_s, own_g, raw_s, raw_r, a_s, a_r, as_s, as_r, f_s, f_r, fs_s, fs_r, zd_s, zd_r, zc_s, zc_r,
    s1_s, s1_r, st_s, st_r, ex_s, ex_r, w_s, w_r, x_s, x_r, far_s, far_r, cx_s, cx_r, s2_s, s2_r,
):
    node, y = lax.axis_index("node"), lax.axis_index("local")
    c, chip = node % 2, node // 2
    x, z = chip // NZ, chip % NZ

    def send(src, dst, ss, rs, to_chip, to_core=None, to_y=None):
        core = c if to_core is None else to_core
        return pltpu.make_async_remote_copy(
            src_ref=src, dst_ref=dst, send_sem=ss, recv_sem=rs,
            device_id=(to_chip * 2 + core, y if to_y is None else to_y), device_id_type=MESH,
        )

    def start(src, dst, ss, rs, to_chip, to_core=None, to_y=None):
        send(src, dst, ss, rs, to_chip, to_core, to_y).start()

    def arrived(ref, sem):
        pltpu.make_async_copy(ref, ref, sem).wait()

    barrier = pltpu.get_barrier_semaphore()

    def greet(to_chip, to_core, to_y):
        pl.semaphore_signal(barrier, inc=1, device_id=(to_chip * 2 + to_core, to_y), device_id_type=MESH)

    greet(chip, 1 - c, y)
    for d in range(1, NX):
        greet((x + d) % NX * NZ + z, c, y)
    for d in range(1, NZ):
        greet(x * NZ + (z + d) % NZ, c, y)
    for d in range(1, NY):
        greet(chip, c, (y + d) % NY)

    scalars = [
        pltpu.make_async_copy(src, dst, sc_s.at[a])
        for a, (src, dst) in enumerate(((ob_in, ob), (nb_in, nb), (steps_in, step_count), (rate_in, learning_rate)))
    ]
    for copy in scalars:
        copy.start()
    state_in = [pltpu.make_async_copy(old.at[0], olds.at[a], in_s.at[a]) for a, old in enumerate((om, of, os_))]
    for copy in state_in:
        copy.start()
    row = lax.broadcasted_iota(I32, (16, WIDTH), 0)
    tail[...] = jnp.where(row < 12, end[0].astype(F32), 0.0).astype(BF16)

    @pl.when(c == 0)
    def _():
        pltpu.make_async_copy(g.at[0, 0:HALF], mine_g, own_g).start()

    @pl.when(c == 1)
    def _():
        pltpu.make_async_copy(g.at[0, SECOND:448], mine_g.at[0:224], own_g).start()
        mine_g[224:240] = tail[...]

    for copy in state_in:
        copy.wait()

    def stage(t, carry):
        col = pl.ds(pl.multiple_of(t * LANE, LANE), LANE)
        for a in range(3):
            stg[t, a] = olds[a, :, col]
        return carry

    lax.fori_loop(0, TILES, stage, 0)
    for t in range(TILES, CHIPS):
        total[t] = jnp.zeros((HALF, LANE), F32)

    pl.semaphore_wait(barrier, 1 + NX - 1 + NZ - 1 + NY - 1)

    @pl.when(c == 0)
    def _():
        for k, (first, rows) in enumerate(CHUNKS):
            rows = min(rows, 224 - first)
            send(g.at[0, SECOND + first : SECOND + first + rows], raw.at[first : first + rows], raw_s.at[k], raw_r.at[k], chip, 1).start()
        send(tail, raw.at[224:240], raw_s.at[NC - 1], raw_r.at[NC - 1], chip, 1).start()

    @pl.when(c == 1)
    def _():
        for k, (first, rows) in enumerate(CHUNKS):
            send(g.at[0, first : first + rows], raw.at[first : first + rows], raw_s.at[k], raw_r.at[k], chip, 0).start()

    @pl.when(c == 0)
    def _():
        pltpu.make_async_copy(mine_g, mine_g, own_g).wait()

    @pl.when(c == 1)
    def _():
        pltpu.make_async_copy(mine_g.at[0:224], mine_g.at[0:224], own_g).wait()

    for d in range(1, NX):
        pl.semaphore_signal(col_s, inc=1, device_id=(((x + d) % NX * NZ + z) * 2 + c, y), device_id_type=MESH)

    pl.semaphore_wait(col_s, NX - 1)

    def state_out(d, carry):
        to = (chip + d) % CHIPS

        @pl.when(to < TILES)
        def _():
            send(stg.at[to], st.at[c, chip], s1_s, s1_r, to).start()

        return carry

    lax.fori_loop(1, CHIPS, state_out, 0)

    @pl.when(chip < TILES)
    def _():
        pltpu.make_async_copy(stg.at[chip], st.at[c, chip], s1_r).start()

    right_x, left_x, far_x = (x + 1) % NX, (x + 3) % NX, (x + 2) % NX
    right_chip, left_chip = right_x * NZ + z, left_x * NZ + z

    def pair(k):
        first, rows = CHUNKS[k]
        at = slice(first, first + rows)
        arrived(raw.at[at], raw_r.at[k])

        def add(t, top):
            col = pl.ds(pl.multiple_of(t * LANE, LANE), LANE)
            value = mine_g[at, col].astype(F32) + raw[at, col].astype(F32)
            total[t, at] = value
            return jnp.maximum(top, jnp.abs(value))

        top = lax.fori_loop(0, TILES, add, jnp.zeros((rows, LANE), F32))
        top = jnp.maximum(jnp.max(top, axis=0, keepdims=True), 1e-30)
        scl[k] = top / LEVEL
        inverse = LEVEL / top

        def code(t, carry):
            acode[t, at] = encode(total[far_x * NZ + t, at], inverse)
            return carry

        lax.fori_loop(0, NZ, code, 0)
        start(acode.at[0:4, at], a_in.at[0, :, at], a_s, a_r.at[k], right_chip)
        start(acode.at[4:8, at], a_in.at[1, :, at], a_s, a_r.at[k], left_chip)
        start(scl.at[k], sa.at[0, k], as_s, as_r.at[k], right_chip)
        start(scl.at[k], sa.at[1, k], as_s, as_r.at[k], left_chip)

    def neighbours(k):
        first, rows = CHUNKS[k]
        at = slice(first, first + rows)
        arrived(a_in.at[:, :, at], a_r.at[k])
        arrived(sa.at[:, k], as_r.at[k])
        rscl[k] = scl[k] + sa[0, k]
        lscl[k] = scl[k] + sa[1, k]
        to_right, to_left = 1.0 / rscl[k], 1.0 / lscl[k]

        def code(t, carry):
            through = decode(a_in[0, t, at], sa[0, k])
            right_code[t, at] = encode(total[right_x * NZ + t, at] + through, to_right)
            right_code[t + 4, at] = encode(total[right_x * NZ + t + 4, at], to_right)
            through = decode(a_in[1, t, at], sa[1, k])
            left_code[t, at] = encode(total[left_x * NZ + t, at], to_left)
            left_code[t + 4, at] = encode(total[left_x * NZ + t + 4, at] + through, to_left)
            return carry

        lax.fori_loop(0, 4, code, 0)
        start(right_code.at[:, at], f_in.at[0, :, at], f_s, f_r.at[k], right_chip)
        start(left_code.at[:, at], f_in.at[1, :, at], f_s, f_r.at[k], left_chip)
        start(rscl.at[k], sf.at[0, k], fs_s, fs_r.at[k], right_chip)
        start(lscl.at[k], sf.at[1, k], fs_s, fs_r.at[k], left_chip)

    def along_z(k):
        first, rows = CHUNKS[k]
        at = slice(first, first + rows)
        arrived(f_in.at[:, :, at], f_r.at[k])
        arrived(sf.at[:, k], fs_r.at[k])
        zscl[k] = scl[k] + sf[0, k] + sf[1, k]
        inverse = 1.0 / zscl[k]

        def code(t, carry):
            value = total[x * NZ + t, at] + decode(f_in[0, t, at], sf[0, k]) + decode(f_in[1, t, at], sf[1, k])
            zsum[t, at] = value
            zsnd[t, at] = encode(value, inverse)
            return carry

        lax.fori_loop(0, NZ, code, 0)
        for d in (1, 7, 2, 6, 3, 5, 4):
            gz = (z + d) % NZ
            to = x * NZ + gz
            start(zsnd.at[gz, at], zr.at[d - 1, at], zd_s, zd_r.at[k], to)
            start(zscl.at[k], zs.at[d - 1, k], zc_s, zc_r.at[k], to)

    pair(0)
    pair(1)
    neighbours(0)
    pair(2)
    neighbours(1)

    along_z(0)
    pair(3)
    neighbours(2)
    along_z(1)
    neighbours(3)
    along_z(2)

    @pl.when(chip < TILES)
    def _():
        arrived(st.at[c], s1_r)

    start(st.at[c], st.at[c], st_s, st_r, chip, 1 - c)
    along_z(3)
    for copy in scalars:
        copy.wait()

    arrived(st.at[1 - c], st_r)
    for a in range(3):
        new[a, 464:480] = jnp.zeros((16, LANE), F32)

    def owner_of(s, i):
        return jnp.minimum(i + (ob[i + 1] <= 4 * s).astype(I32), NODES - 1)

    def place(s, i):
        i = owner_of(s, i)
        offset = jnp.clip(4 * s - ob[i], 0, 4)
        for a in range(3):
            mat[a, pl.ds(4 * s, 4)] = st[i % 2, i // 2, a, pl.ds(offset, 4)]
        return i

    before = lax.fori_loop(0, c * (SECOND // 4), owner_of, jnp.int32(0))
    lax.fori_loop(c * (SECOND // 4), c * (SECOND // 4) + HALF // 4, place, before)

    for k, (first, rows) in enumerate(CHUNKS):
        at = slice(first, first + rows)
        arrived(zr.at[:, at], zd_r.at[k])
        arrived(zs.at[:, k], zc_r.at[k])
        value = zsum[z, at]
        for d in range(NZ - 1):
            value = value + decode(zr[d, at], zs[d, k])
        grad[at] = value

    steps = step_count[0]
    rate = learning_rate[0]
    first_left = 1.0 - power(beta_first, steps)
    second_left = 1.0 - power(beta_second, steps)

    def step(b, carry):
        rows = pl.ds(pl.multiple_of(c * SECOND + b * 48, 16), 48)
        gradient = grad[pl.ds(pl.multiple_of(b * 48, 16), 48)]
        master = mat[0, rows]
        first_new = beta_first * mat[1, rows] + (1.0 - beta_first) * gradient
        second_new = beta_second * mat[2, rows] + (1.0 - beta_second) * gradient * gradient
        first_hat = first_new / first_left
        second_hat = second_new / second_left
        new[0, rows] = master - rate * (first_hat / (jnp.sqrt(second_hat) + adam_eps) + decay * master)
        new[1, rows] = first_new
        new[2, rows] = second_new
        return carry

    lax.fori_loop(0, HALF // 48, step, 0)

    for i in range(2):
        rows = new[0, pl.ds(c * 230 + 115 * i, 120)]
        wb[i] = jnp.concatenate([rows, jnp.zeros((8, LANE), F32)], axis=0).astype(BF16)
    for dz in (0, 1, 7, 2, 6, 3, 5, 4):
        for i in range(2):
            yy = 2 * c + i
            to = x * NZ + (z + dz) % NZ
            for other in range(2):
                core = (c + other) % 2
                src = wb.at[i, pl.ds(pl.multiple_of(core * PART, PART), PART)]
                dst = blocks.at[core, x, z, y]
                if dz == 0 and other == 0:
                    @pl.when(yy == y)
                    def _():
                        pltpu.make_async_copy(src, dst, w_r.at[0]).start()

                    @pl.when(yy != y)
                    def _():
                        start(src, dst, w_s, w_r.at[0], to, core, yy)
                else:
                    start(src, dst, w_s, w_r.at[dz], to, core, yy)

    @pl.when(c == 0)
    def _():
        send(new.at[:, 0:224], peer, ex_s, ex_r, chip, 1).start()

    @pl.when(c == 1)
    def _():
        send(new.at[:, 240:464], peer, ex_s, ex_r, chip, 0).start()

    arrived(peer, ex_r)
    theirs = pl.ds(pl.multiple_of((1 - c) * HALF, 16), 224)
    for a in range(3):
        new[a, theirs] = peer[a]

    def pick(m, carry):
        begin = jnp.clip(nb[2 * m + c], 0, UNITS)
        count = nb[2 * m + c + 1] - begin
        slot = lax.broadcasted_iota(I32, (CAP_NEW, LANE), 0)
        for a in range(3):
            rows = new[a, pl.ds(begin, CAP_NEW)]
            snd[m, CAP_NEW * a : CAP_NEW * (a + 1)] = jnp.where(slot < count, rows, 0.0)
        return carry

    lax.fori_loop(0, OWNERS // 2, pick, 0)

    def share(ref):
        start(ref, ref, cx_s, cx_r, chip, 1 - c)

    def spread(at, e):
        ref = blocks.at[c, x, at]
        start(ref, ref, x_s, x_r.at[0, e], right_chip)
        start(ref, ref, x_s, x_r.at[1, e], left_chip)
        share(ref)

    def relay(at, e):
        arrived(blocks.at[c, left_x, at], x_r.at[0, e])
        half = blocks.at[c, left_x, at, 0:2]
        start(half, half, far_s, far_r.at[e], right_chip)
        arrived(blocks.at[c, right_x, at], x_r.at[1, e])
        half = blocks.at[c, right_x, at, 2:4]
        start(half, half, far_s, far_r.at[e], left_chip)
        share(blocks.at[c, left_x, at])
        share(blocks.at[c, right_x, at])

    owner = (48 - c - chip) % CHIPS

    def owners_out(d, carry):
        to = (chip + d) % CHIPS
        m = (48 - c - to) % CHIPS

        @pl.when((m < OWNERS // 2) & (chip < TILES))
        def _():
            send(snd.at[m], r2.at[chip], s2_s, s2_r, to).start()

        return carry

    @pl.when((owner < OWNERS // 2) & (chip < TILES))
    def _():
        pltpu.make_async_copy(snd.at[owner], r2.at[chip], s2_r).start()

    lax.fori_loop(1, CHIPS, owners_out, 0)

    order = (0, 1, 7, 2, 6, 3, 5, 4)
    for n, dz in enumerate(order):
        at = (z + NZ - dz) % NZ
        arrived(blocks.at[c, x, at], w_r.at[dz])
        spread(at, dz)
        if n >= 2:
            relay((z + NZ - order[n - 2]) % NZ, order[n - 2])

    for dz in order[6:]:
        relay((z + NZ - dz) % NZ, dz)

    for dz in order:
        ref = blocks.at[c, far_x, (z + NZ - dz) % NZ]
        arrived(ref, far_r.at[dz])
        share(ref)

    @pl.when(owner < OWNERS // 2)
    def _():
        arrived(r2.at[0:TILES], s2_r)

    @pl.when(owner >= OWNERS // 2)
    def _():
        zero[...] = jnp.zeros_like(zero)
        clear = pltpu.make_async_copy(zero, r2.at[0:TILES], s2_r)
        clear.start()
        clear.wait()

    @pl.when((owner < OWNERS // 2) & (chip < TILES))
    def _():
        arrived(snd.at[0:25], s2_s)

    @pl.when((owner >= OWNERS // 2) & (chip < TILES))
    def _():
        arrived(snd.at[0:26], s2_s)

    arrived(blocks.at[1 - c], cx_r)
    for k, (first, rows) in enumerate(CHUNKS):
        arrived(raw.at[first : first + rows], raw_s.at[k])

    @pl.when(chip < TILES)
    def _():
        arrived(stg.at[0:28], s1_s)

    @pl.when(chip >= TILES)
    def _():
        arrived(stg.at[0:29], s1_s)

    @pl.when(y // 2 != c)
    def _():
        arrived(blocks.at[c, 0], w_s)

    @pl.when(y // 2 == c)
    def _():
        arrived(total.at[0:31, 0:32], w_s)

    for ref, sem in (
        (acode, a_s), (sa, as_s), (f_in, f_s), (sf, fs_s), (zr, zd_s), (zs, zc_s), (st.at[c], st_s),
        (peer, ex_s), (blocks.at[c, 0:2], x_s), (blocks.at[c, 0], far_s), (blocks.at[c], cx_s),
    ):
        arrived(ref, sem)


def lay_out(blocks, r2, o_m, o_f, o_s, o_w, got, rows, state, wide, in_s, out_s):
    here = pltpu.make_async_copy(r2, rows, in_s.at[NY])
    here.start()
    copies = [pltpu.make_async_copy(blocks.at[:, :, :, q], got.at[q], in_s.at[q]) for q in range(NY)]
    for copy in copies:
        copy.start()
    outs = []

    def out(src, dst):
        outs.append(pltpu.make_async_copy(src, dst, out_s.at[len(outs)]))
        outs[-1].start()

    here.wait()

    def tile(t, carry):
        for a in range(3):
            for s in range(CAP_NEW):
                state[a, s, t] = rows[t, CAP_NEW * a + s : CAP_NEW * a + s + 1]
        return carry

    lax.fori_loop(0, TILES, tile, 0)
    for a, dst in enumerate((o_m, o_f, o_s)):
        out(state.at[a], dst)
    for q in range(NY):
        copies[q].wait()
        for t in range(TILES):
            col = slice(t * LANE, (t + 1) * LANE)
            wide[q, 0:64, col] = got[q, 0, t // NZ, t % NZ]
            wide[q, 64:115, col] = got[q, 1, t // NZ, t % NZ, 0:51]
        out(wide.at[q], o_w.at[:, q * WIDTH : (q + 1) * WIDTH])
    for copy in outs:
        copy.wait()


def on_device(grad_partials, old_master, old_first, old_second, old_bounds, new_bounds, step_count, learning_rate):
    dma = pltpu.SemaphoreType.DMA
    hbm = pl.BlockSpec(memory_space=pl.ANY)
    scale = pltpu.VMEM((NC, 1, LANE), F32)
    scratch = [
        pltpu.SMEM((NODES + 1,), I32),
        pltpu.SMEM((OWNERS + 1,), I32),
        pltpu.SMEM((1,), I32),
        pltpu.SMEM((1,), F32),
        pltpu.VMEM((HALF, WIDTH), BF16),
        pltpu.VMEM((HALF, WIDTH), BF16),
        pltpu.VMEM((16, WIDTH), BF16),
        pltpu.VMEM((3, 8, WIDTH), F32),
        pltpu.VMEM((CHIPS, HALF, LANE), F32),
        pltpu.VMEM((NZ, HALF, LANE), I16),
        pltpu.VMEM((NZ, HALF, LANE), I16),
        pltpu.VMEM((NZ, HALF, LANE), I16),
        scale, scale, scale,
        pltpu.VMEM((2, NZ // 2, HALF, LANE), I16),
        pltpu.VMEM((2, NC, 1, LANE), F32),
        pltpu.VMEM((2, NZ, HALF, LANE), I16),
        pltpu.VMEM((2, NC, 1, LANE), F32),
        pltpu.VMEM((NZ, HALF, LANE), F32),
        pltpu.VMEM((NZ, HALF, LANE), I16),
        scale,
        pltpu.VMEM((NZ - 1, HALF, LANE), I16),
        pltpu.VMEM((NZ - 1, NC, 1, LANE), F32),
        pltpu.VMEM((HALF, LANE), F32),
        pltpu.VMEM((CHIPS, 3, 8, LANE), F32),
        pltpu.VMEM((2, CHIPS, 3, 8, LANE), F32),
        pltpu.VMEM((3, 480, LANE), F32),
        pltpu.VMEM((3, 480, LANE), F32),
        pltpu.VMEM((3, 224, LANE), F32),
        pltpu.VMEM((2, 128, LANE), BF16),
        pltpu.VMEM((OWNERS // 2, 3 * CAP_NEW, LANE), F32),
        pltpu.VMEM((TILES, 3 * CAP_NEW, LANE), F32),
        dma((4,)), pltpu.SemaphoreType.REGULAR,
        dma((3,)), dma,
        dma((NC,)), dma((NC,)),
        dma, dma((NC,)), dma, dma((NC,)), dma, dma((NC,)), dma, dma((NC,)),
        dma, dma((NC,)), dma, dma((NC,)),
        dma, dma, dma, dma, dma, dma,
        dma, dma((NZ,)), dma, dma((2, NZ)), dma, dma((NZ,)), dma, dma,
        dma, dma,
    ]
    blocks, r2 = pl.pallas_call(
        kernel,
        name="adamw_move",
        out_shape=(
            jax.ShapeDtypeStruct((2, NX, NZ, NY, PART, LANE), BF16),
            jax.ShapeDtypeStruct((CHIPS, 3 * CAP_NEW, LANE), F32),
        ),
        in_specs=[hbm, hbm, hbm, hbm, hbm, pl.BlockSpec((1, 16, WIDTH), lambda i: (0, 28, 0)), hbm, hbm, hbm],
        grid=(1,),
        out_specs=(hbm, hbm),
        scratch_shapes=scratch,
        compiler_params=pltpu.CompilerParams(collective_id=0, has_side_effects=True, vmem_limit_bytes=56 * 2**20),
    )(old_bounds, new_bounds, step_count, learning_rate, grad_partials, grad_partials, old_master, old_first, old_second)
    rows = jax.ShapeDtypeStruct((CAP_NEW, TILES, 1, LANE), F32)
    outs = pl.pallas_call(
        lay_out,
        name="lay_out",
        out_shape=(rows, rows, rows, jax.ShapeDtypeStruct((115, NY * WIDTH), BF16)),
        in_specs=[hbm, hbm],
        out_specs=(hbm, hbm, hbm, hbm),
        scratch_shapes=[
            pltpu.VMEM((NY, 2, NX, NZ, PART, LANE), BF16),
            pltpu.VMEM((CHIPS, 3 * CAP_NEW, LANE), F32),
            pltpu.VMEM((3, CAP_NEW, TILES, 1, LANE), F32),
            pltpu.VMEM((NY, 115, WIDTH), BF16),
            dma((NY + 1,)),
            dma((NY + 3,)),
        ],
        compiler_params=pltpu.CompilerParams(vmem_limit_bytes=60 * 2**20),
    )(blocks, r2)
    return tuple(out.reshape(1, CAP_NEW, WIDTH) for out in outs[:3]) + (outs[3],)


def solution(mesh):
    split = P("node", None, "local")
    return jax.shard_map(
        on_device,
        mesh=mesh,
        in_specs=(split, split, split, split, P(), P(), P(), P()),
        out_specs=(split, split, split, P("local", None)),
        check_vma=False,
    )
```
